128 devices in a mesh: pair: 32 (over z, x, y_hi), row: 4 (over y_lo, core).
Axes of the slice: x: 4, y: 4 (y_hi: 2, y_lo: 2; y = y_hi * 2 + y_lo), z: 4, core: 2. Of those that a mesh axis runs over, the one named last changes fastest.
Arguments:
- samples_slab: float32 [4, 8192, 8192], P('row', 'pair'), may hold values from -420 to 420
- block_order: int32 [128], replicated, may hold values from 0 to 127, each once
- rotations: float32 [3, 64, 128, 128], P(None, 'pair'), may hold values from -0.5 to 0.5
Outputs:
- rotated_slab: float32 [8192, 32768], P('pair', 'row')
- pair_grams: float32 [3, 64, 128, 128], P(None, 'pair')
The draws below stay inside these ranges and needn't reach their ends.
Inputs may be any that keep to these rules, and one draw needn't show every extreme that they name: `block_order`: each block number appears once.
All inputs are finite; a program needn't handle non-finite values.
Results may differ from the reference program's by a relative error of at most 0.0003.
Values sent between devices are 32-bit elements; how exact they have to be, the bound alone decides.
No kernel may reach another device: no remote copies, remote signals or barrier semaphores. Data moves between devices by JAX's collectives and lax.ppermute only.
A program may use at most 192 MiB of HBM per device.

```python
import math
import jax
import jax.numpy as jnp
from jax import lax

NCOL = 8192
BLOCK = 64
STEPS = 3
NBLK = 128
NPAIR = 64
PAIRW = 128
SAMPLES = 8192
ROWS = 32768
N_ROW = 4


def draw_samples_slab(key, part):
    key = jax.random.fold_in(key, 1)
    key_base, key_col, key_row = jax.random.split(key, 3)
    shape = (N_ROW, SAMPLES, NCOL)
    col_scale = jnp.exp(jax.random.uniform(key_col, (NCOL,), jnp.float32, 0.0, math.log(10.0)))
    row_scale = jnp.exp(jax.random.uniform(key_row, (N_ROW, SAMPLES, 1), jnp.float32, 0.0, math.log(10.0)))
    base = jax.random.truncated_normal(key_base, -4.0, 4.0, shape, jnp.float32)
    return base * col_scale * row_scale


def block_levels(rng, extent, cuts, low, largest):
    level = 1.0
    for position, shards_of in cuts:
        heights = jax.random.uniform(jax.random.fold_in(jax.random.fold_in(rng, 6), position), (shards_of,), jnp.float32, low / len(cuts), largest / len(cuts))
        level = level * jnp.repeat(jnp.exp(heights), extent[position] // shards_of).reshape((-1,) + (1,) * (len(extent) - 1 - position))
    return level


def normal_values(key, extent, spread, most, cuts=(), dtype=jnp.bfloat16):
    entries = spread * jax.random.normal(key, extent, jnp.float32)
    if cuts:
        entries = entries * block_levels(key, extent, cuts, -0.22, 0.18)
    return jnp.clip(entries, -most, most).astype(dtype)


def setup_inputs(seed: int = 0) -> dict:
    keys = jax.random.split(jax.random.key(seed), 4)
    samples_slab = draw_samples_slab(jax.random.fold_in(keys[3], 71), 0)
    block_order = jax.random.permutation(keys[1], NBLK).astype(jnp.int32)
    rotations = normal_values(keys[2], (STEPS, NPAIR, PAIRW, PAIRW), PAIRW ** -0.5, 0.5, ((1, 32),), jnp.float32)
    return dict(samples_slab=samples_slab, block_order=block_order, rotations=rotations)


epsilon = 1e-06

def sandwich(mixing, gram_sum):
    inner = jnp.einsum('kce,kef->kcf', gram_sum, mixing, precision=lax.Precision.HIGHEST)
    return jnp.einsum('kcd,kcf->kdf', mixing, inner, precision=lax.Precision.HIGHEST)

def assemble(upper_blocks, lower_blocks, upper_chain, incoming_upper, incoming_lower, at_start, at_end):
    first_upper = jnp.where(at_start, upper_blocks[0], incoming_upper)
    new_upper = jnp.concatenate([first_upper[None], upper_chain[:-1]], 0)
    last_lower = jnp.where(at_end, upper_blocks[-1], incoming_lower)
    new_lower = jnp.concatenate([lower_blocks[1:], last_lower[None]], 0)
    return jnp.stack([new_upper, new_lower], 1)

def upper_sequence(upper_blocks, lower_blocks, at_start):
    head = jnp.where(at_start, lower_blocks[0], upper_blocks[0])
    return jnp.concatenate([head[None], upper_blocks[1:]], 0)

def reference(samples_slab, block_order, rotations):
    matrix = samples_slab.reshape(ROWS, NCOL).T.reshape(NBLK, BLOCK, ROWS)
    columns_held = jnp.take(matrix, block_order, axis=0).reshape(NPAIR, 2, BLOCK, ROWS)
    results = []
    for turn_index in range(STEPS):
        pair_cols = columns_held.reshape(NPAIR, PAIRW, ROWS)
        gram_sum = jnp.einsum('kcr,kdr->kcd', pair_cols, pair_cols, precision=lax.Precision.HIGHEST)
        diagonal_sum = jnp.diagonal(gram_sum, axis1=1, axis2=2)
        inverse_norm = lax.rsqrt(diagonal_sum / ROWS + epsilon)
        mixing = rotations[turn_index] * inverse_norm[:, :, None]
        mixed_cols = jnp.einsum('kcd,kcr->kdr', mixing, pair_cols, precision=lax.Precision.HIGHEST)
        results.append(sandwich(mixing, gram_sum) / ROWS)
        columns_held = mixed_cols.reshape(NPAIR, 2, BLOCK, ROWS)
        if turn_index + 1 < STEPS:
            upper_blocks = columns_held[:, 0]
            lower_blocks = columns_held[:, 1]
            upper_chain = upper_sequence(upper_blocks, lower_blocks, True)
            columns_held = assemble(upper_blocks, lower_blocks, upper_chain, upper_blocks[0], lower_blocks[0], True, True)
    return (columns_held.reshape(NCOL, ROWS), jnp.stack(results))
```

```python
import functools
import itertools

import jax
import jax.numpy as jnp
from jax import lax
from jax.experimental import pallas as pl
from jax.experimental.pallas import tpu as pltpu
from jax.sharding import PartitionSpec as P


BOTH = ("pair", "row")
NZ, NX, NY, NC = 4, 4, 2, 2
NPAIR = 64
PAIRW = 128
HALF = 64
SAMP = 256
NDEV = 32
ROWS = 32768
EPS = 1e-06
QUARTER = 24
PAYROWS = 256 + QUARTER + 32
MIB = 1 << 20
F32, BF16 = jnp.float32, jnp.bfloat16


def flat(z, x, yh, yl, c):
    return (((z * NX + x) * 2 + yh) * 2 + yl) * 2 + c


def exchange(value, flip):
    pairs = []
    for here in itertools.product(range(NZ), range(NX), range(2), range(2), range(2)):
        there = tuple(a ^ b for a, b in zip(here, flip))
        pairs.append((flat(*here), flat(*there)))
    return lax.ppermute(value, BOTH, pairs)


def sum_all(value):
    for flip in (
        (0, 0, 0, 0, 1),
        (0, 0, 0, 1, 0),
        (0, 0, 1, 1, 0),
        (0, 1, 0, 0, 0),
        (0, 3, 0, 0, 0),
        (1, 0, 0, 0, 0),
        (3, 0, 0, 0, 0),
    ):
        value = value + exchange(value, flip)
    return value


def sum_row(value):
    for flip in ((0, 0, 0, 0, 1), (0, 0, 0, 1, 0)):
        value = value + exchange(value, flip)
    return value


def gather_pairs(own):
    def grow(held, offs, flip, bit):
        return jnp.concatenate([held, exchange(held, flip)], 0), offs + [o ^ bit for o in offs]

    x1, x3, z1, z3 = (0, 1, 0, 0, 0), (0, 3, 0, 0, 0), (1, 0, 0, 0, 0), (3, 0, 0, 0, 0)
    first, first_offs = own, [0]
    second, second_offs = exchange(own, (0, 0, 1, 1, 0)), [2]
    first, first_offs = grow(first, first_offs, x1, 4)
    second, second_offs = grow(second, second_offs, z1, 16)
    first, first_offs = grow(first, first_offs, x3, 12)
    second, second_offs = grow(second, second_offs, z3, 48)
    first, first_offs = grow(first, first_offs, z1, 16)
    second, second_offs = grow(second, second_offs, x1, 4)
    pieces = [first, exchange(first, z3), second, exchange(second, x3)]
    offs = [first_offs, [o ^ 48 for o in first_offs], second_offs, [o ^ 12 for o in second_offs]]
    for k in range(4):
        pieces.append(exchange(pieces[k], (0, 0, 0, 0, 1)))
        offs.append([o ^ 1 for o in offs[k]])
    return pieces, sum(offs, [])


def split(value):
    high = value.astype(BF16)
    return high, (value - high.astype(F32)).astype(BF16)


def left_operand(mixing_t):
    high, low = split(mixing_t)
    return jnp.concatenate(
        [
            jnp.concatenate([high, high], 1),
            jnp.concatenate([low, jnp.zeros_like(low)], 1),
        ],
        0,
    )


def product(left, right):
    wide = jnp.dot(left, right, preferred_element_type=F32)
    return wide[:PAIRW] + wide[PAIRW:]


def outer(a, b):
    return lax.dot_general(a, b, (((1,), (1,)), ((), ())), preferred_element_type=F32)


def self_gram(stacked):
    wide = outer(stacked, stacked)
    return wide[:PAIRW, :PAIRW] + wide[PAIRW:, :PAIRW] + wide[:PAIRW, PAIRW:]


def diagonal_row(gram):
    size = gram.shape[0]
    eye = lax.broadcasted_iota(jnp.int32, (size, size), 0) == lax.broadcasted_iota(
        jnp.int32, (size, size), 1
    )
    return jnp.sum(jnp.where(eye, gram, 0.0), axis=0, keepdims=True)


def scales(norm_row):
    return lax.rsqrt(norm_row / ROWS + EPS)


def lanes(shape):
    return lax.broadcasted_iota(jnp.int32, shape, 1)


def next_slots(i):
    upper = jnp.where(i == 0, 0, jnp.where(i == NPAIR - 1, 2 * NPAIR - 1, 2 * i + 2))
    lower = jnp.where(i == 0, 2, 2 * i - 1)
    return upper, lower


def prepare_kernel(x_ref, norm_ref, high_ref, low_ref):
    tiles = x_ref.shape[1] // PAIRW
    for t in range(tiles):
        tile = x_ref[:, t * PAIRW : (t + 1) * PAIRW]
        norm_ref[t : t + 1, :] = jnp.sum(tile * tile, axis=0, keepdims=True)
        high, low = split(tile.T)
        high_ref[2 * t] = high[:HALF]
        high_ref[2 * t + 1] = high[HALF:]
        low_ref[2 * t] = low[:HALF]
        low_ref[2 * t + 1] = low[HALF:]


def prepare(x):
    width = 1024
    steps = x.shape[1] // width
    blocks = width // HALF
    spec = pl.BlockSpec((blocks, HALF, SAMP), lambda g: (g, 0, 0))
    halves = jax.ShapeDtypeStruct((2 * NPAIR, HALF, SAMP), BF16)
    return pl.pallas_call(
        prepare_kernel,
        grid=(steps,),
        in_specs=[pl.BlockSpec((SAMP, width), lambda g: (0, g))],
        out_specs=[pl.BlockSpec((width // PAIRW, PAIRW), lambda g: (g, 0)), spec, spec],
        out_shape=[jax.ShapeDtypeStruct((NPAIR, PAIRW), F32), halves, halves],
        compiler_params=pltpu.CompilerParams(vmem_limit_bytes=32 * MIB),
        cost_estimate=pl.CostEstimate(flops=8 * MIB, bytes_accessed=16 * MIB, transcendentals=0),
        name="prepare",
    )(x)


def step0_kernel(tab_ref, order_ref, place_ref, norm_ref, high_ref, low_ref, *rest):
    pieces, rest = rest[:8], rest[8:]
    ohigh_ref, olow_ref, keep_ref, send_ref, onorm_ref, rot_ref, norms_ref, sems = rest
    copies = [
        pltpu.make_async_copy(piece, rot_ref.at[pl.ds(8 * k, 8)], sems.at[k])
        for k, piece in enumerate(pieces)
    ]
    for copy in copies:
        copy.start()
    norms_ref[0] = norm_ref[...]
    norms_ref[1] = pltpu.roll(norm_ref[...], HALF, 1)
    core, y_lo = place_ref[0], place_ref[1]
    for copy in copies:
        copy.wait()

    def one(q):
        i = tab_ref[q]
        bu, bl = order_ref[2 * i], order_ref[2 * i + 1]
        nu = norms_ref[bu % 2, pl.ds(bu // 2, 1), :]
        nl = norms_ref[1 - bl % 2, pl.ds(bl // 2, 1), :]
        scale = scales(jnp.where(lanes((1, PAIRW)) < HALF, nu, nl))
        left = left_operand(rot_ref[q] * scale)
        right = jnp.concatenate([high_ref[bu], high_ref[bl], low_ref[bu], low_ref[bl]], 0)
        moved = product(left, right)
        high, low = split(moved)
        su, sl = next_slots(i)
        ohigh_ref[su] = high[:HALF]
        ohigh_ref[sl] = high[HALF:]
        olow_ref[su] = low[:HALF]
        olow_ref[sl] = low[HALF:]
        gram = self_gram(jnp.concatenate([high, low], 0))
        onorm_ref[pl.ds(i, 1), :] = diagonal_row(gram)
        bottom = gram[HALF:]
        packed = jnp.where(
            lanes((32, PAIRW)) >= HALF, bottom[:32], pltpu.roll(bottom[32:], HALF, 1)
        )
        quarters = [
            gram[0:24],
            gram[24:48],
            jnp.concatenate([gram[48:64], packed[0:8]], 0),
            packed[8:32],
        ]
        mine = core == 0
        for yy in range(2):
            even, odd = quarters[2 * yy], quarters[2 * yy + 1]
            keep_ref[yy ^ y_lo, i] = jnp.where(mine, even, odd)
            send_ref[yy ^ y_lo, i] = jnp.where(mine, odd, even)

    def several(g, carry):
        for k in range(4):
            one(4 * g + k)
        return carry

    lax.fori_loop(0, NPAIR // 4, several, 0)


def step0(tab, order, place, norms, high, low, pieces):
    smem = pl.BlockSpec(memory_space=pltpu.SMEM)
    vmem = pl.BlockSpec(memory_space=pltpu.VMEM)
    halves = jax.ShapeDtypeStruct((2 * NPAIR, HALF, SAMP), BF16)
    grams = jax.ShapeDtypeStruct((2, NPAIR, QUARTER, PAIRW), F32)
    return pl.pallas_call(
        step0_kernel,
        in_specs=[smem] * 3 + [vmem] * 3 + [pl.BlockSpec(memory_space=pl.ANY)] * 8,
        out_specs=[vmem] * 5,
        out_shape=[halves, halves, grams, grams, jax.ShapeDtypeStruct((NPAIR, PAIRW), F32)],
        scratch_shapes=[
            pltpu.VMEM((NPAIR, PAIRW, PAIRW), F32),
            pltpu.VMEM((2, NPAIR, PAIRW), F32),
            pltpu.SemaphoreType.DMA((8,)),
        ],
        compiler_params=pltpu.CompilerParams(vmem_limit_bytes=36 * MIB),
        cost_estimate=pl.CostEstimate(flops=4 << 30, bytes_accessed=24 * MIB, transcendentals=0),
        name="step0",
    )(tab, order, place, norms, high, low, *pieces)


def step1_kernel(norm_ref, high_ref, low_ref, rot_ref, gram_ref, pay_ref, norms_ref):
    norms_ref[0] = norm_ref[...]
    norms_ref[1] = pltpu.roll(norm_ref[...], HALF, 1)

    def one(p, j):
        i = 2 * p + j
        nu = norms_ref[jnp.where(i == 1, 1, 0), pl.ds(jnp.maximum(i - 1, 0), 1), :]
        nl = norms_ref[
            jnp.where(i == NPAIR - 1, 1, 0), pl.ds(jnp.minimum(i + 1, NPAIR - 1), 1), :
        ]
        scale = scales(jnp.where(lanes((1, PAIRW)) < HALF, nu, nl))
        left = left_operand(rot_ref[i] * scale)
        right = jnp.concatenate(
            [high_ref[2 * i], high_ref[2 * i + 1], low_ref[2 * i], low_ref[2 * i + 1]], 0
        )
        moved = product(left, right)
        su, sl = next_slots(i)
        pay_ref[su // 4, pl.ds(pl.multiple_of((su % 4) * HALF, HALF), HALF), :] = moved[:HALF]
        pay_ref[sl // 4, pl.ds(pl.multiple_of((sl % 4) * HALF, HALF), HALF), :] = moved[HALF:]
        high, low = split(moved)
        wide = outer(
            jnp.concatenate([high[:HALF], low[:HALF]], 0),
            jnp.concatenate([high[HALF:], low[HALF:]], 0),
        )
        folded = wide[:HALF] + wide[HALF:]
        folded = folded + pltpu.roll(folded, HALF, 1)
        cross = jnp.where(lanes((32, PAIRW)) < HALF, folded[:32], folded[32:])
        here = slice(j * PAIRW, (j + 1) * PAIRW)
        pay_ref[p, 256 : 256 + QUARTER, here] = gram_ref[i]
        pay_ref[p, 256 + QUARTER : PAYROWS, here] = cross

    def several(g, carry):
        for k in range(4):
            one(2 * g + k // 2, k % 2)
        return carry

    lax.fori_loop(0, NPAIR // 4, several, 0)


def step1(norms, high, low, rot, gram):
    vmem = pl.BlockSpec(memory_space=pltpu.VMEM)
    return pl.pallas_call(
        step1_kernel,
        in_specs=[vmem] * 5,
        out_specs=vmem,
        out_shape=jax.ShapeDtypeStruct((NDEV, PAYROWS, SAMP), F32),
        scratch_shapes=[pltpu.VMEM((2, NPAIR, PAIRW), F32)],
        compiler_params=pltpu.CompilerParams(vmem_limit_bytes=36 * MIB),
        cost_estimate=pl.CostEstimate(flops=3 << 30, bytes_accessed=24 * MIB, transcendentals=0),
        name="step1",
    )(norms, high, low, rot, gram)


def gram2_kernel(y_ref, gram_ref, sums_ref):
    @pl.when(pl.program_id(0) == 0)
    def _():
        gram_ref[...] = jnp.zeros_like(gram_ref)
        sums_ref[...] = jnp.zeros_like(sums_ref)

    count = y_ref.shape[0]
    for j in range(2):
        tiles = [split(y_ref[s, j * PAIRW : (j + 1) * PAIRW, :]) for s in range(count)]
        stacked = jnp.concatenate([jnp.concatenate(t, 0) for t in tiles], 1)
        gram_ref[j] += self_gram(stacked)
    sums_ref[...] += sum(y_ref[s, 256:PAYROWS, :] for s in range(count))


def gram2(y):
    count = 4
    return pl.pallas_call(
        gram2_kernel,
        grid=(NDEV // count,),
        in_specs=[pl.BlockSpec((count, PAYROWS, SAMP), lambda g: (g, 0, 0))],
        out_specs=[
            pl.BlockSpec((2, PAIRW, PAIRW), lambda g: (0, 0, 0)),
            pl.BlockSpec((PAYROWS - 256, SAMP), lambda g: (0, 0)),
        ],
        out_shape=[
            jax.ShapeDtypeStruct((2, PAIRW, PAIRW), F32),
            jax.ShapeDtypeStruct((PAYROWS - 256, SAMP), F32),
        ],
        compiler_params=pltpu.CompilerParams(vmem_limit_bytes=24 * MIB),
        cost_estimate=pl.CostEstimate(flops=2 << 30, bytes_accessed=10 * MIB, transcendentals=0),
        name="gram2",
    )(y)


def step2_kernel(gram_ref, rot_ref, y_ref, out_ref, pg_ref):
    count = y_ref.shape[0]
    mixings = [rot_ref[j] * scales(diagonal_row(gram_ref[j])) for j in range(2)]
    for j in range(2):
        left = left_operand(mixings[j])
        for s in range(count):
            right = jnp.concatenate(split(y_ref[s, j * PAIRW : (j + 1) * PAIRW, :]), 0)
            out_ref[j * PAIRW : (j + 1) * PAIRW, s * SAMP : (s + 1) * SAMP] = product(left, right)

    @pl.when(pl.program_id(0) == 0)
    def _():
        for j in range(2):
            inner = jnp.dot(
                mixings[j], gram_ref[j], precision=lax.Precision.HIGHEST, preferred_element_type=F32
            )
            pg_ref[j] = lax.dot_general(
                inner,
                mixings[j],
                (((1,), (1,)), ((), ())),
                precision=lax.Precision.HIGHEST,
                preferred_element_type=F32,
            )


def step2(gram, rot, y):
    count = 4
    whole = pl.BlockSpec((2, PAIRW, PAIRW), lambda g: (0, 0, 0))
    return pl.pallas_call(
        step2_kernel,
        grid=(NDEV // count,),
        in_specs=[whole, whole, pl.BlockSpec((count, 256, SAMP), lambda g: (g, 0, 0))],
        out_specs=[pl.BlockSpec((256, count * SAMP), lambda g: (0, g)), whole],
        out_shape=[
            jax.ShapeDtypeStruct((256, NDEV * SAMP), F32),
            jax.ShapeDtypeStruct((2, PAIRW, PAIRW), F32),
        ],
        compiler_params=pltpu.CompilerParams(vmem_limit_bytes=24 * MIB),
        cost_estimate=pl.CostEstimate(flops=2 << 30, bytes_accessed=18 * MIB, transcendentals=0),
        name="step2",
    )(gram, rot, y)


def grams_kernel(ends_ref, sums_ref, gram_ref, above_ref, below_ref, last_ref, out_ref):
    shape = (HALF, PAIRW)
    left = lanes(shape) < HALF
    zero = jnp.zeros(shape, F32)

    def symmetric(top, bottom):
        full = jnp.concatenate([top, bottom], 0)
        turned = full.T
        low_left = (lanes((PAIRW, PAIRW)) < HALF) & (
            lax.broadcasted_iota(jnp.int32, (PAIRW, PAIRW), 0) >= HALF
        )
        return jnp.where(low_left, turned, full) * (1.0 / ROWS)

    def turn(value):
        return pltpu.roll(value, HALF, 1)

    first, last = ends_ref[0] == 1, ends_ref[1] == 1
    for j in range(2):
        here = slice(j * PAIRW, (j + 1) * PAIRW)
        top = sums_ref[0:64, here]
        packed = sums_ref[64:96, here]
        low = jnp.where(left, zero, jnp.concatenate([packed, turn(packed)], 0))
        out_ref[0, j] = symmetric(top, low)
        packed = sums_ref[96:128, here]
        cross = jnp.concatenate([turn(packed), packed], 0)
        if j == 0:
            upper = jnp.where(first, gram_ref[0, :HALF], gram_ref[1, :HALF])
            lower = jnp.where(first, turn(gram_ref[1, :HALF]), below_ref[...])
        else:
            upper = jnp.where(last, turn(gram_ref[1, HALF:]), above_ref[...])
            lower = gram_ref[0, HALF:]
        out_ref[1, j] = symmetric(jnp.where(left, upper, cross), jnp.where(left, zero, lower))
        out_ref[2, j] = last_ref[j] * (1.0 / ROWS)


def grams(ends, sums, gram, above, below, last):
    vmem = pl.BlockSpec(memory_space=pltpu.VMEM)
    return pl.pallas_call(
        grams_kernel,
        in_specs=[pl.BlockSpec(memory_space=pltpu.SMEM)] + [vmem] * 5,
        out_specs=vmem,
        out_shape=jax.ShapeDtypeStruct((3, 2, PAIRW, PAIRW), F32),
        compiler_params=pltpu.CompilerParams(vmem_limit_bytes=16 * MIB),
        cost_estimate=pl.CostEstimate(flops=1 << 20, bytes_accessed=2 * MIB, transcendentals=0),
        name="grams",
    )(ends, sums, gram, above, below, last)


def body(samples_slab, block_order, rotations):
    pair, row = lax.axis_index("pair"), lax.axis_index("row")
    core, y_lo = row % 2, row // 2
    turned = jnp.swapaxes(rotations, 2, 3)
    own0 = lax.dynamic_slice_in_dim(turned[0], core, 1, 0)
    own1 = lax.dynamic_slice_in_dim(turned[1].reshape(4, HALF, PAIRW), row, 1, 0)
    rot1 = lax.all_gather(own1, BOTH, axis=0, tiled=True).reshape(NPAIR, PAIRW, PAIRW)
    pieces, offs = gather_pairs(own0)
    tab = (2 * pair + core) ^ jnp.array(offs, jnp.int32)
    norm0, high, low = prepare(samples_slab[0])
    norm0 = sum_all(norm0)
    place = jnp.stack([core, y_lo]).astype(jnp.int32)
    high, low, keep, send, norm1 = step0(tab, block_order, place, norm0, high, low, pieces)
    norm1 = sum_all(norm1)
    keep = keep + exchange(send, (0, 0, 0, 0, 1))
    quarter = keep[0] + exchange(keep[1], (0, 0, 0, 1, 0))
    payload = step1(norm1, high, low, rot1, quarter)
    arrived = lax.all_to_all(payload, "pair", 0, 0)
    gram, sums = gram2(arrived)
    gram = sum_row(gram)
    placed = lax.dynamic_update_slice(
        jnp.zeros((4 * QUARTER, SAMP), F32), sums[:QUARTER], (row * QUARTER, 0)
    )
    sums = sum_row(jnp.concatenate([placed, sums[QUARTER:]], 0))
    above = lax.ppermute(gram[0, :HALF], "pair", [(k, k - 1) for k in range(1, NDEV)])
    below = lax.ppermute(gram[1, HALF:], "pair", [(k - 1, k) for k in range(1, NDEV)])
    rotated, last = step2(gram, turned[2], arrived)
    ends = jnp.stack([pair == 0, pair == NDEV - 1]).astype(jnp.int32)
    return rotated, grams(ends, sums, gram, above, below, last)


def solution(mesh):
    in_specs = (P("row", "pair", None), P(), P(None, "pair", None, None))
    out_specs = (P("pair", "row"), P(None, "pair", None, None))
    return jax.shard_map(body, mesh=mesh, in_specs=in_specs, out_specs=out_specs, check_vma=False)
```

```python
import functools
import itertools

import jax
import jax.numpy as jnp
from jax import lax
from jax.experimental import pallas as pl
from jax.experimental.pallas import tpu as pltpu
from jax.sharding import PartitionSpec as P


BOTH = ("pair", "row")
NZ, NX, NY, NC = 4, 4, 2, 2
NPAIR = 64
PAIRW = 128
HALF = 64
SAMP = 256
NDEV = 32
ROWS = 32768
EPS = 1e-06
QUARTER = 32
PAYROWS = 256 + QUARTER
MIB = 1 << 20
F32, BF16 = jnp.float32, jnp.bfloat16


def flat(z, x, yh, yl, c):
    return (((z * NX + x) * 2 + yh) * 2 + yl) * 2 + c


def exchange(value, flip):
    pairs = []
    for here in itertools.product(range(NZ), range(NX), range(2), range(2), range(2)):
        there = tuple(a ^ b for a, b in zip(here, flip))
        pairs.append((flat(*here), flat(*there)))
    return lax.ppermute(value, BOTH, pairs)


X1, X3, Z1, Z3 = (0, 1, 0, 0, 0), (0, 3, 0, 0, 0), (1, 0, 0, 0, 0), (3, 0, 0, 0, 0)
YLO, YBOTH, CORE = (0, 0, 0, 1, 0), (0, 0, 1, 1, 0), (0, 0, 0, 0, 1)


def add_over(value, *flips):
    for flip in flips:
        value = value + exchange(value, flip)
    return value


def together(*values):
    return lax.optimization_barrier(values)


def split(value):
    high = value.astype(BF16)
    return high, (value - high.astype(F32)).astype(BF16)


def left_operand(mixing_t):
    high, low = split(mixing_t)
    return jnp.concatenate(
        [
            jnp.concatenate([high, high], 1),
            jnp.concatenate([low, jnp.zeros_like(low)], 1),
        ],
        0,
    )


def product(left, right):
    wide = jnp.dot(left, right, preferred_element_type=F32)
    return wide[:PAIRW] + wide[PAIRW:]


def outer(a, b):
    return lax.dot_general(a, b, (((1,), (1,)), ((), ())), preferred_element_type=F32)


def self_gram(stacked):
    wide = outer(stacked, stacked)
    return wide[:PAIRW, :PAIRW] + wide[PAIRW:, :PAIRW] + wide[:PAIRW, PAIRW:]


def diagonal_row(gram):
    size = gram.shape[0]
    eye = lax.broadcasted_iota(jnp.int32, (size, size), 0) == lax.broadcasted_iota(
        jnp.int32, (size, size), 1
    )
    return jnp.sum(jnp.where(eye, gram, 0.0), axis=0, keepdims=True)


def scales(norm_row):
    return lax.rsqrt(norm_row / ROWS + EPS)


def lanes(shape):
    return lax.broadcasted_iota(jnp.int32, shape, 1)


def next_slots(i):
    upper = jnp.where(i == 0, 0, jnp.where(i == NPAIR - 1, 2 * NPAIR - 1, 2 * i + 2))
    lower = jnp.where(i == 0, 2, 2 * i - 1)
    return upper, lower


TILES = NPAIR // 2


def norms_kernel(place_ref, x_ref, norm_ref, held_ref, sems):
    count = sems.shape[0]
    width = NPAIR // count

    def copy(g):
        part = pl.ds(g * width * PAIRW, width * PAIRW)
        return pltpu.make_async_copy(x_ref.at[:, part], held_ref.at[:, part], sems.at[g])

    for g in range(count):
        copy(g).start()
    for g in range(count):
        copy(g).wait()
        for t in range(width * g, width * (g + 1)):
            tile = held_ref[:, t * PAIRW : (t + 1) * PAIRW]
            row = jnp.sum(tile * tile, axis=0, keepdims=True)
            norm_ref[(t // TILES) ^ place_ref[2], t % TILES : t % TILES + 1, :] = row


def norms(place, x):
    return pl.pallas_call(
        norms_kernel,
        in_specs=[pl.BlockSpec(memory_space=pltpu.SMEM), pl.BlockSpec(memory_space=pl.ANY)],
        out_specs=pl.BlockSpec(memory_space=pltpu.VMEM),
        out_shape=jax.ShapeDtypeStruct((2, TILES, PAIRW), F32),
        scratch_shapes=[pltpu.VMEM((SAMP, NPAIR * PAIRW), F32), pltpu.SemaphoreType.DMA((8,))],
        compiler_params=pltpu.CompilerParams(vmem_limit_bytes=58 * MIB),
        cost_estimate=pl.CostEstimate(flops=8 * MIB, bytes_accessed=8 * MIB, transcendentals=0),
        name="norms",
    )(place, x)


def prepare_kernel(x_ref, halves_ref):
    tiles = x_ref.shape[1] // PAIRW
    for t in range(tiles):
        tile = x_ref[:, t * PAIRW : (t + 1) * PAIRW]
        high, low = split(tile.T)
        for h in range(2):
            halves_ref[2 * t + h, 0] = high[h * HALF : (h + 1) * HALF]
            halves_ref[2 * t + h, 1] = low[h * HALF : (h + 1) * HALF]


def prepare(x):
    width = 1024
    blocks = width // HALF
    return pl.pallas_call(
        prepare_kernel,
        grid=(x.shape[1] // width,),
        in_specs=[pl.BlockSpec((SAMP, width), lambda g: (0, g))],
        out_specs=pl.BlockSpec((blocks, 2, HALF, SAMP), lambda g: (g, 0, 0, 0)),
        out_shape=jax.ShapeDtypeStruct((2 * NPAIR, 2, HALF, SAMP), BF16),
        compiler_params=pltpu.CompilerParams(vmem_limit_bytes=58 * MIB),
        cost_estimate=pl.CostEstimate(flops=8 * MIB, bytes_accessed=16 * MIB, transcendentals=0),
        name="prepare",
    )(x)


SENT = PAIRW + TILES


def spread_kernel(place_ref, rot_ref, norm_ref, given_ref, copies_ref, quarter_ref, turned_ref):
    row, core = place_ref[0], place_ref[2]
    own = rot_ref[0, core].T
    norm = norm_ref[0] + given_ref[...]

    def copy(k, carry):
        copies_ref[k, :PAIRW] = own
        copies_ref[k, PAIRW:] = norm
        return carry

    lax.fori_loop(0, NDEV, copy, 0, unroll=4)
    for t in range(1, 3):
        for j in range(2):
            turned_ref[t - 1, j] = rot_ref[t, j].T
    half = pl.ds(pl.multiple_of((row % 2) * HALF, HALF), HALF)
    quarter_ref[...] = turned_ref[0, row // 2, half, :]


def spread(place, rotations, norm, given):
    vmem = pl.BlockSpec(memory_space=pltpu.VMEM)
    return pl.pallas_call(
        spread_kernel,
        in_specs=[pl.BlockSpec(memory_space=pltpu.SMEM), vmem, vmem, vmem],
        out_specs=[vmem] * 3,
        out_shape=[
            jax.ShapeDtypeStruct((NDEV, SENT, PAIRW), F32),
            jax.ShapeDtypeStruct((HALF, PAIRW), F32),
            jax.ShapeDtypeStruct((2, 2, PAIRW, PAIRW), F32),
        ],
        compiler_params=pltpu.CompilerParams(vmem_limit_bytes=8 * MIB),
        cost_estimate=pl.CostEstimate(flops=MIB, bytes_accessed=3 * MIB, transcendentals=0),
        name="spread",
    )(place, rotations, norm, given)


def collect_kernel(arrived_ref, norm_ref):
    norm_ref[...] = sum(arrived_ref[s, PAIRW:] for s in range(NDEV))


def collect(arrived):
    vmem = pl.BlockSpec(memory_space=pltpu.VMEM)
    return pl.pallas_call(
        collect_kernel,
        in_specs=[vmem],
        out_specs=vmem,
        out_shape=jax.ShapeDtypeStruct((TILES, PAIRW), F32),
        compiler_params=pltpu.CompilerParams(vmem_limit_bytes=8 * MIB),
        cost_estimate=pl.CostEstimate(flops=MIB, bytes_accessed=MIB, transcendentals=0),
        name="collect",
    )(arrived)


GROUP = 8
GROUPS = NPAIR // GROUP
OPERAND = (NPAIR, 2, 2, HALF, SAMP)


def whole_copy(ref, sem):
    return pltpu.make_async_copy(ref, ref, sem)


def step0_kernel(
    tab_ref, order_ref, place_ref, normc_ref, normo_ref, halves_ref, mine_ref, given_ref,
    next_ref, parts_ref, onorm_ref, right_ref, rot_ref, moved_ref, norms_ref, sems, out_sem
):

    def fetch(q, carry):
        i = tab_ref[q]
        for h in range(2):
            pltpu.make_async_copy(
                halves_ref.at[order_ref[2 * i + h]], right_ref.at[q, :, h], sems.at[0, q // GROUP]
            ).start()
        return carry

    lax.fori_loop(0, NPAIR, fetch, 0)
    for k in range(GROUPS):
        piece = (mine_ref, given_ref)[k // 4].at[pl.ds(GROUP * (k % 4), GROUP), pl.ds(0, PAIRW)]
        pltpu.make_async_copy(piece, rot_ref.at[pl.ds(GROUP * k, GROUP)], sems.at[1, k]).start()
    core = place_ref[2]
    for half, norm_ref in ((core, normc_ref), (1 - core, normo_ref)):
        rows = pl.ds(pl.multiple_of(half * TILES, TILES), TILES)
        norms_ref[0, rows, :] = norm_ref[...]
        norms_ref[1, rows, :] = pltpu.roll(norm_ref[...], HALF, 1)

    def spot(quarter, j):
        mine = quarter ^ place_ref[j]
        return (mine & 1) * 2 + (mine >> 1)

    def group(g, carry):
        part = pl.ds(GROUP * g, GROUP)
        whole_copy(right_ref.at[part], sems.at[0, g]).wait()
        whole_copy(rot_ref.at[part], sems.at[1, g]).wait()
        todo = [GROUP * g + k for k in range(GROUP)]
        index = [tab_ref[q] for q in todo]
        lefts = []
        for q, i in zip(todo, index):
            bu, bl = order_ref[2 * i], order_ref[2 * i + 1]
            nu = norms_ref[bu % 2, pl.ds(bu // 2, 1), :]
            nl = norms_ref[1 - bl % 2, pl.ds(bl // 2, 1), :]
            scale = scales(jnp.where(lanes((1, PAIRW)) < HALF, nu, nl))
            lefts.append(left_operand(rot_ref[q] * scale))
        values = [
            split(product(left, right_ref[q].reshape(2 * PAIRW, SAMP)))
            for left, q in zip(lefts, todo)
        ]
        for i, pieces_of in zip(index, values):
            slots = next_slots(i)
            for part_of, value in enumerate(pieces_of):
                for h, slot in enumerate(slots):
                    moved_ref[slot // 2, part_of, slot % 2] = value[h * HALF : (h + 1) * HALF]
        for i, (high, low) in zip(index, values):
            gram = self_gram(jnp.concatenate([high, low], 0))
            onorm_ref[pl.ds(i, 1), :] = diagonal_row(gram)
            bottom = gram[HALF:]
            packed = jnp.where(
                lanes((32, PAIRW)) >= HALF, bottom[:32], pltpu.roll(bottom[32:], HALF, 1)
            )
            p, j = i // 2, i % 2
            parts_ref[spot(0, j), j, p] = gram[:32]
            parts_ref[spot(1, j), j, p] = gram[32:HALF]
            parts_ref[spot(2, j), j, p] = packed
        return carry

    lax.fori_loop(0, GROUPS, group, 0)
    copy = pltpu.make_async_copy(moved_ref, next_ref, out_sem)
    copy.start()

    def cross(g, carry):
        wides = []
        for k in range(GROUP):
            upper = moved_ref[GROUP * g + k, :, 0].reshape(PAIRW, SAMP)
            lower = moved_ref[GROUP * g + k, :, 1].reshape(PAIRW, SAMP)
            wides.append(outer(upper, lower))
        for k, wide in enumerate(wides):
            folded = wide[:HALF] + wide[HALF:]
            folded = folded + pltpu.roll(folded, HALF, 1)
            parts_ref[spot(3, k % 2), k % 2, GROUP // 2 * g + k // 2] = jnp.where(
                lanes((32, PAIRW)) < HALF, folded[:32], folded[32:]
            )
        return carry

    lax.fori_loop(0, GROUPS, cross, 0)
    copy.wait()


def step0(tab, order, place, normc, normo, halves, mine, given):
    smem = pl.BlockSpec(memory_space=pltpu.SMEM)
    vmem = pl.BlockSpec(memory_space=pltpu.VMEM)
    anywhere = pl.BlockSpec(memory_space=pl.ANY)
    return pl.pallas_call(
        step0_kernel,
        in_specs=[smem] * 3 + [vmem] * 2 + [anywhere] * 3,
        out_specs=[anywhere, vmem, vmem],
        out_shape=[
            jax.ShapeDtypeStruct(OPERAND, BF16),
            jax.ShapeDtypeStruct((4, 2, NDEV, QUARTER, PAIRW), F32),
            jax.ShapeDtypeStruct((NPAIR, PAIRW), F32),
        ],
        scratch_shapes=[
            pltpu.VMEM(OPERAND, BF16),
            pltpu.VMEM((NPAIR, PAIRW, PAIRW), F32),
            pltpu.VMEM(OPERAND, BF16),
            pltpu.VMEM((2, NPAIR, PAIRW), F32),
            pltpu.SemaphoreType.DMA((2, GROUPS)),
            pltpu.SemaphoreType.DMA,
        ],
        compiler_params=pltpu.CompilerParams(vmem_limit_bytes=44 * MIB),
        cost_estimate=pl.CostEstimate(flops=4 << 30, bytes_accessed=24 * MIB, transcendentals=0),
        name="step0",
    )(tab, order, place, normc, normo, halves, mine, given)


def step1_kernel(
    norm_ref, operand_ref, rotation_ref, parta_ref, partb_ref, pay_ref, right_ref, rot_ref,
    norms_ref, sems
):
    for g in range(GROUPS):
        part = pl.ds(GROUP * g, GROUP)
        pltpu.make_async_copy(operand_ref.at[part], right_ref.at[part], sems.at[0, g]).start()
        pltpu.make_async_copy(rotation_ref.at[part], rot_ref.at[part], sems.at[1, g]).start()
    norms_ref[0] = norm_ref[...]
    norms_ref[1] = pltpu.roll(norm_ref[...], HALF, 1)
    pay_ref[:, 256:PAYROWS, :PAIRW] = parta_ref[...]
    pay_ref[:, 256:PAYROWS, PAIRW:] = partb_ref[...]

    def group(g, carry):
        part = pl.ds(GROUP * g, GROUP)
        whole_copy(right_ref.at[part], sems.at[0, g]).wait()
        whole_copy(rot_ref.at[part], sems.at[1, g]).wait()
        index = [GROUP * g + k for k in range(GROUP)]
        lefts = []
        for i in index:
            nu = norms_ref[jnp.where(i == 1, 1, 0), pl.ds(jnp.maximum(i - 1, 0), 1), :]
            nl = norms_ref[
                jnp.where(i == NPAIR - 1, 1, 0), pl.ds(jnp.minimum(i + 1, NPAIR - 1), 1), :
            ]
            scale = scales(jnp.where(lanes((1, PAIRW)) < HALF, nu, nl))
            lefts.append(left_operand(rot_ref[i] * scale))
        values = [
            product(left, right_ref[i].reshape(2 * PAIRW, SAMP)) for left, i in zip(lefts, index)
        ]
        for i, value in zip(index, values):
            for h, slot in enumerate(next_slots(i)):
                spot = pl.ds(pl.multiple_of((slot % 4) * HALF, HALF), HALF)
                pay_ref[slot // 4, spot, :] = value[h * HALF : (h + 1) * HALF]
        return carry

    lax.fori_loop(0, GROUPS, group, 0)


def step1(norm, operand, rot, parta, partb):
    vmem = pl.BlockSpec(memory_space=pltpu.VMEM)
    anywhere = pl.BlockSpec(memory_space=pl.ANY)
    return pl.pallas_call(
        step1_kernel,
        in_specs=[vmem, anywhere, anywhere, vmem, vmem],
        out_specs=vmem,
        out_shape=jax.ShapeDtypeStruct((NDEV, PAYROWS, SAMP), F32),
        scratch_shapes=[
            pltpu.VMEM(OPERAND, BF16),
            pltpu.VMEM((NPAIR, PAIRW, PAIRW), F32),
            pltpu.VMEM((2, NPAIR, PAIRW), F32),
            pltpu.SemaphoreType.DMA((2, GROUPS)),
        ],
        compiler_params=pltpu.CompilerParams(vmem_limit_bytes=28 * MIB),
        cost_estimate=pl.CostEstimate(flops=3 << 30, bytes_accessed=24 * MIB, transcendentals=0),
        name="step1",
    )(norm, operand, rot, parta, partb)


CHUNK = 4
CHUNKS = NDEV // CHUNK


def parts_kernel(place_ref, y_ref, placed_ref):
    sums = []
    for z_odd in range(2):
        source = [s for s in range(NDEV) if (s // (2 * NX)) % 2 == z_odd]
        sums.append(sum(y_ref[s, 256:PAYROWS, :] for s in source))
    placed_ref[...] = jnp.zeros_like(placed_ref)
    row, core = place_ref[0], place_ref[2]
    spots = [pl.ds(pl.multiple_of(QUARTER * q, QUARTER), QUARTER) for q in (row, core, core + 2)]
    placed_ref[0, spots[0], :] = sums[0][:, :PAIRW] + sums[1][:, :PAIRW]
    placed_ref[1, spots[1], :] = sums[0][:, PAIRW:]
    placed_ref[1, spots[2], :] = sums[1][:, PAIRW:]


def parts(place, y):
    vmem = pl.BlockSpec(memory_space=pltpu.VMEM)
    return pl.pallas_call(
        parts_kernel,
        in_specs=[pl.BlockSpec(memory_space=pltpu.SMEM), vmem],
        out_specs=vmem,
        out_shape=jax.ShapeDtypeStruct((2, 4 * QUARTER, PAIRW), F32),
        compiler_params=pltpu.CompilerParams(vmem_limit_bytes=14 * MIB),
        cost_estimate=pl.CostEstimate(flops=MIB, bytes_accessed=MIB, transcendentals=0),
        name="parts",
    )(place, y)


def gram2_kernel(y_ref, norm_ref, gram_ref):
    totals = [None, None]
    for g in range(CHUNKS):
        source = range(CHUNK * g, CHUNK * (g + 1))
        for j in range(2):
            halves = [split(y_ref[s, j * PAIRW : (j + 1) * PAIRW, :]) for s in source]
            high = jnp.concatenate([h for h, _ in halves], 1)
            low = jnp.concatenate([l for _, l in halves], 1)
            term = outer(high, jnp.concatenate([high, low], 0))
            totals[j] = term if g == 0 else totals[j] + term
    for j in range(2):
        mixed = totals[j][:, PAIRW:]
        gram = totals[j][:, :PAIRW] + mixed + mixed.T
        gram_ref[j] = gram
        norm_ref[j] = jnp.broadcast_to(diagonal_row(gram), (8, PAIRW))


def gram2(y):
    vmem = pl.BlockSpec(memory_space=pltpu.VMEM)
    return pl.pallas_call(
        gram2_kernel,
        in_specs=[vmem],
        out_specs=[vmem, vmem],
        out_shape=[
            jax.ShapeDtypeStruct((2, 8, PAIRW), F32),
            jax.ShapeDtypeStruct((2, PAIRW, PAIRW), F32),
        ],
        compiler_params=pltpu.CompilerParams(vmem_limit_bytes=14 * MIB),
        cost_estimate=pl.CostEstimate(flops=2 << 30, bytes_accessed=10 * MIB, transcendentals=0),
        name="gram2",
    )(y)


def step2_kernel(norm_ref, rot_ref, y_ref, out_ref, turned_ref, out_sem):
    lefts = [left_operand(rot_ref[j] * scales(norm_ref[j, 0:1])) for j in range(2)]
    for g in range(CHUNKS):
        for j in range(2):
            here = slice(j * PAIRW, (j + 1) * PAIRW)
            for s in range(CHUNK * g, CHUNK * (g + 1)):
                right = jnp.concatenate(split(y_ref[s, here, :]), 0)
                turned_ref[here, s * SAMP : (s + 1) * SAMP] = product(lefts[j], right)
        part = pl.ds(CHUNK * SAMP * g, CHUNK * SAMP)
        pltpu.make_async_copy(turned_ref.at[:, part], out_ref.at[:, part], out_sem).start()
    whole_copy(turned_ref, out_sem).wait()


def step2(norm, rot, y):
    vmem = pl.BlockSpec(memory_space=pltpu.VMEM)
    return pl.pallas_call(
        step2_kernel,
        in_specs=[vmem, vmem, vmem],
        out_specs=pl.BlockSpec(memory_space=pl.ANY),
        out_shape=jax.ShapeDtypeStruct((256, NDEV * SAMP), F32),
        scratch_shapes=[pltpu.VMEM((2 * PAIRW, NDEV * SAMP), F32), pltpu.SemaphoreType.DMA],
        compiler_params=pltpu.CompilerParams(vmem_limit_bytes=24 * MIB),
        cost_estimate=pl.CostEstimate(flops=2 << 30, bytes_accessed=18 * MIB, transcendentals=0),
        name="step2",
    )(norm, rot, y)


def sandwich(mixing_t, gram):
    inner = jnp.dot(
        mixing_t, gram, precision=lax.Precision.HIGHEST, preferred_element_type=F32
    )
    return lax.dot_general(
        inner,
        mixing_t,
        (((1,), (1,)), ((), ())),
        precision=lax.Precision.HIGHEST,
        preferred_element_type=F32,
    )


def grams_kernel(place_ref, rows_ref, rot1_ref, rot2_ref, out_ref):
    sums = [rows_ref[256:384], rows_ref[384:512]]
    below, above = rows_ref[512:576], rows_ref[576:608]
    shape = (HALF, PAIRW)
    left = lanes(shape) < HALF
    zero = jnp.zeros(shape, F32)

    def turn(value):
        return pltpu.roll(value, HALF, 1)

    def unpack(packed):
        return jnp.concatenate([packed, turn(packed)], 0)

    def symmetric(upper, cross, lower):
        full = jnp.concatenate([jnp.where(left, upper, cross), jnp.where(left, zero, lower)], 0)
        low_left = (lanes((PAIRW, PAIRW)) < HALF) & (
            lax.broadcasted_iota(jnp.int32, (PAIRW, PAIRW), 0) >= HALF
        )
        return jnp.where(low_left, full.T, full)

    first, last = place_ref[3] == 1, place_ref[4] == 1
    tops = [part[0:64] for part in sums]
    lows = [unpack(part[64:96]) for part in sums]
    for j in range(2):
        out_ref[0, j] = symmetric(tops[j], tops[j], lows[j]) * (1.0 / ROWS)
        packed = sums[j][96:128]
        cross = jnp.concatenate([turn(packed), packed], 0)
        if j == 0:
            upper = jnp.where(first, tops[0], below)
            lower = lows[1]
        else:
            upper = jnp.where(first, turn(lows[0]), tops[0])
            lower = jnp.where(last, turn(tops[1]), unpack(above))
        gram = symmetric(upper, cross, lower)
        for t, rot, full in ((1, rot1_ref[j], gram), (2, rot2_ref[j], rows_ref[j * PAIRW : (j + 1) * PAIRW])):
            out_ref[t, j] = sandwich(rot * scales(diagonal_row(full)), full) * (1.0 / ROWS)


def grams(place, rows, rot1, rot2):
    vmem = pl.BlockSpec(memory_space=pltpu.VMEM)
    return pl.pallas_call(
        grams_kernel,
        in_specs=[pl.BlockSpec(memory_space=pltpu.SMEM)] + [vmem] * 3,
        out_specs=vmem,
        out_shape=jax.ShapeDtypeStruct((3, 2, PAIRW, PAIRW), F32),
        compiler_params=pltpu.CompilerParams(vmem_limit_bytes=16 * MIB),
        cost_estimate=pl.CostEstimate(flops=1 << 20, bytes_accessed=2 * MIB, transcendentals=0),
        name="grams",
    )(place, rows, rot1, rot2)


def body(samples_slab, block_order, rotations):
    pair, row = lax.axis_index("pair"), lax.axis_index("row")
    core = row % 2
    z_odd = (pair // (NX * 2)) % 2
    place = jnp.stack([row, 2 * z_odd + core, core, pair == 0, pair == NDEV - 1]).astype(jnp.int32)
    even = 2 * jnp.arange(NDEV, dtype=jnp.int32)
    tab = jnp.concatenate([even + core, even + (1 - core)])
    x = samples_slab[0]
    norm0 = norms(place, x)
    copies, quarter1, turned = spread(place, rotations, norm0, exchange(norm0[1], CORE))
    rot1 = lax.all_gather(quarter1, BOTH, axis=0, tiled=True).reshape(NPAIR, PAIRW, PAIRW)
    mine = lax.all_to_all(copies, "pair", 0, 0)
    halves = prepare(x)
    mine, halves = together(mine, halves)
    theirs = exchange(mine, CORE)
    norm0 = add_over(collect(mine), YLO)
    operand, given, norm1 = step0(
        tab, block_order, place, norm0, exchange(norm0, CORE), halves, mine, theirs
    )
    kept = given[:2] + exchange(given[2:], CORE)
    norm1 = add_over(norm1, Z1, YLO)
    kept, _ = together(kept, norm1)
    quarters = [kept[0, j] + exchange(kept[1, j], flip) for j, flip in enumerate((YLO, Z1))]
    norm1 = add_over(norm1, Z3, YBOTH, X1, X3, CORE)
    payload = step1(norm1, operand, rot1, *quarters)
    arrived = lax.all_to_all(payload, "pair", 0, 0)
    sums = parts(place, arrived)
    arrived, sums = together(arrived, sums)
    below = lax.ppermute(sums[1, :HALF], "pair", [(k, k + 1) for k in range(NDEV - 1)])
    above = lax.ppermute(sums[0, 64:96], "pair", [(k + 1, k) for k in range(NDEV - 1)])
    norm2, gram = gram2(arrived)
    rows = [gram.reshape(2 * PAIRW, PAIRW), sums.reshape(2 * PAIRW, PAIRW), below, above]
    norm2 = add_over(norm2, CORE)
    rows = add_over(jnp.concatenate(rows, 0), CORE)
    norm2 = add_over(norm2, YLO)
    norm2, rows = together(norm2, rows)
    rows = add_over(rows, YLO)
    rotated = step2(norm2, turned[1], arrived)
    return rotated, grams(place, rows, turned[0], turned[1])


def solution(mesh):
    in_specs = (P("row", "pair", None), P(), P(None, "pair", None, None))
    out_specs = (P("pair", "row"), P(None, "pair", None, None))
    return jax.shard_map(body, mesh=mesh, in_specs=in_specs, out_specs=out_specs, check_vma=False)
```

```python
import functools
import itertools

import jax
import jax.numpy as jnp
from jax import lax
from jax.experimental import pallas as pl
from jax.experimental.pallas import tpu as pltpu
from jax.sharding import PartitionSpec as P


BOTH = ("pair", "row")
NZ, NX, NY, NC = 4, 4, 2, 2
NPAIR = 64
PAIRW = 128
HALF = 64
SAMP = 256
NDEV = 32
ROWS = 32768
EPS = 1e-06
QUARTER = 24
PAYROWS = 256 + QUARTER
MIB = 1 << 20
F32, BF16 = jnp.float32, jnp.bfloat16


def flat(z, x, yh, yl, c):
    return (((z * NX + x) * 2 + yh) * 2 + yl) * 2 + c


def exchange(value, flip):
    pairs = []
    for here in itertools.product(range(NZ), range(NX), range(2), range(2), range(2)):
        there = tuple(a ^ b for a, b in zip(here, flip))
        pairs.append((flat(*here), flat(*there)))
    return lax.ppermute(value, BOTH, pairs)


X1, X3, Z1, Z3 = (0, 1, 0, 0, 0), (0, 3, 0, 0, 0), (1, 0, 0, 0, 0), (3, 0, 0, 0, 0)
YLO, YBOTH, CORE = (0, 0, 0, 1, 0), (0, 0, 1, 1, 0), (0, 0, 0, 0, 1)


def add_over(value, *flips):
    for flip in flips:
        value = value + exchange(value, flip)
    return value


def together(*values):
    return lax.optimization_barrier(values)


def split(value):
    high = value.astype(BF16)
    return high, (value - high.astype(F32)).astype(BF16)


def left_operand(mixing_t):
    high, low = split(mixing_t)
    return jnp.concatenate(
        [
            jnp.concatenate([high, high], 1),
            jnp.concatenate([low, jnp.zeros_like(low)], 1),
        ],
        0,
    )


def product(left, right):
    wide = jnp.dot(left, right, preferred_element_type=F32)
    return wide[:PAIRW] + wide[PAIRW:]


def outer(a, b):
    return lax.dot_general(a, b, (((1,), (1,)), ((), ())), preferred_element_type=F32)


def self_gram(stacked):
    wide = outer(stacked, stacked)
    return wide[:PAIRW, :PAIRW] + wide[PAIRW:, :PAIRW] + wide[:PAIRW, PAIRW:]


def diagonal_row(gram):
    size = gram.shape[0]
    eye = lax.broadcasted_iota(jnp.int32, (size, size), 0) == lax.broadcasted_iota(
        jnp.int32, (size, size), 1
    )
    return jnp.sum(jnp.where(eye, gram, 0.0), axis=0, keepdims=True)


def scales(norm_row):
    return lax.rsqrt(norm_row / ROWS + EPS)


def lanes(shape):
    return lax.broadcasted_iota(jnp.int32, shape, 1)


def upper_or_diagonal(rows=HALF):
    shape = (rows, PAIRW)
    return lax.broadcasted_iota(jnp.int32, shape, 0) <= lanes(shape)


def next_slots(i):
    upper = jnp.where(i == 0, 0, jnp.where(i == NPAIR - 1, 2 * NPAIR - 1, 2 * i + 2))
    lower = jnp.where(i == 0, 2, 2 * i - 1)
    return upper, lower


TILES = NPAIR // 2


def norms_kernel(
    place_ref, x_ref, rotations_ref, keep_ref, give_ref, own_ref, quarter_ref, turned_ref,
    held_ref, rot_ref, rows_ref, sems, rot_sem
):
    count = sems.shape[0]
    width = NPAIR // count

    def copy(g):
        part = pl.ds(g * width * PAIRW, width * PAIRW)
        return pltpu.make_async_copy(x_ref.at[:, part], held_ref.at[:, part], sems.at[g])

    rot_copy = pltpu.make_async_copy(rotations_ref, rot_ref, rot_sem)
    rot_copy.start()
    for g in range(count):
        copy(g).start()
    row, core = place_ref[0], place_ref[2]
    rot_copy.wait()
    own_ref[...] = rot_ref[0, core].T
    for t in range(1, 3):
        for j in range(2):
            turned_ref[t - 1, j] = rot_ref[t, j].T
    half = pl.ds(pl.multiple_of((row % 2) * HALF, HALF), HALF)
    quarter_ref[...] = turned_ref[0, row // 2, half, :]
    for g in range(count):
        copy(g).wait()
        for t in range(width * g, width * (g + 1)):
            tile = held_ref[:, t * PAIRW : (t + 1) * PAIRW]
            rows_ref[t // TILES, t % TILES : t % TILES + 1, :] = jnp.sum(
                tile * tile, axis=0, keepdims=True
            )
    keep_ref[...] = rows_ref[core]
    give_ref[...] = rows_ref[1 - core]


def norms(place, x, rotations):
    vmem = pl.BlockSpec(memory_space=pltpu.VMEM)
    hbm = pl.BlockSpec(memory_space=pltpu.HBM)
    return pl.pallas_call(
        norms_kernel,
        in_specs=[pl.BlockSpec(memory_space=pltpu.SMEM), hbm, hbm],
        out_specs=[vmem] * 5,
        out_shape=[
            jax.ShapeDtypeStruct((TILES, PAIRW), F32),
            jax.ShapeDtypeStruct((TILES, PAIRW), F32),
            jax.ShapeDtypeStruct((PAIRW, PAIRW), F32),
            jax.ShapeDtypeStruct((HALF, PAIRW), F32),
            jax.ShapeDtypeStruct((2, 2, PAIRW, PAIRW), F32),
        ],
        scratch_shapes=[
            pltpu.VMEM((SAMP, NPAIR * PAIRW), F32),
            pltpu.VMEM((3, 2, PAIRW, PAIRW), F32),
            pltpu.VMEM((2, TILES, PAIRW), F32),
            pltpu.SemaphoreType.DMA((8,)),
            pltpu.SemaphoreType.DMA,
        ],
        compiler_params=pltpu.CompilerParams(vmem_limit_bytes=58 * MIB),
        cost_estimate=pl.CostEstimate(flops=8 * MIB, bytes_accessed=8 * MIB, transcendentals=0),
        name="norms",
    )(place, x, rotations)


def prepare_kernel(x_ref, halves_ref):
    tiles = x_ref.shape[1] // PAIRW
    for t in range(tiles):
        tile = x_ref[:, t * PAIRW : (t + 1) * PAIRW]
        high, low = split(tile.T)
        for h in range(2):
            halves_ref[2 * t + h, 0] = high[h * HALF : (h + 1) * HALF]
            halves_ref[2 * t + h, 1] = low[h * HALF : (h + 1) * HALF]


def prepare(x):
    width = 1024
    blocks = width // HALF
    return pl.pallas_call(
        prepare_kernel,
        grid=(x.shape[1] // width,),
        in_specs=[pl.BlockSpec((SAMP, width), lambda g: (0, g))],
        out_specs=pl.BlockSpec((blocks, 2, HALF, SAMP), lambda g: (g, 0, 0, 0)),
        out_shape=jax.ShapeDtypeStruct((2 * NPAIR, 2, HALF, SAMP), BF16),
        compiler_params=pltpu.CompilerParams(vmem_limit_bytes=58 * MIB),
        cost_estimate=pl.CostEstimate(flops=MIB, bytes_accessed=MIB // 8, transcendentals=0),
        name="prepare",
    )(x)


SENT = PAIRW + TILES


def spread_kernel(own_ref, norm_ref, given_ref, copies_ref):
    own = own_ref[...]
    norm = norm_ref[...] + given_ref[...]

    def copy(k, carry):
        copies_ref[k, :PAIRW] = own
        copies_ref[k, PAIRW:] = norm
        return carry

    lax.fori_loop(0, NDEV, copy, 0, unroll=4)


def spread(own, norm, given):
    vmem = pl.BlockSpec(memory_space=pltpu.VMEM)
    return pl.pallas_call(
        spread_kernel,
        in_specs=[vmem] * 3,
        out_specs=vmem,
        out_shape=jax.ShapeDtypeStruct((NDEV, SENT, PAIRW), F32),
        compiler_params=pltpu.CompilerParams(vmem_limit_bytes=58 * MIB),
        cost_estimate=pl.CostEstimate(flops=MIB, bytes_accessed=MIB // 8, transcendentals=0),
        name="spread",
    )(own, norm, given)


def collect_kernel(arrived_ref, norm_ref):
    norm_ref[...] = sum(arrived_ref[s, PAIRW:] for s in range(NDEV))


def collect(arrived):
    vmem = pl.BlockSpec(memory_space=pltpu.VMEM)
    return pl.pallas_call(
        collect_kernel,
        in_specs=[vmem],
        out_specs=vmem,
        out_shape=jax.ShapeDtypeStruct((TILES, PAIRW), F32),
        compiler_params=pltpu.CompilerParams(vmem_limit_bytes=8 * MIB),
        cost_estimate=pl.CostEstimate(flops=MIB, bytes_accessed=MIB // 8, transcendentals=0),
        name="collect",
    )(arrived)


GROUP = 8
GROUPS = NPAIR // GROUP
OPERAND = (NPAIR, 2, 2, HALF, SAMP)
ROOM = 4


def whole_copy(ref, sem):
    return pltpu.make_async_copy(ref, ref, sem)


def step0_kernel(
    tab_ref, order_ref, place_ref, normc_ref, normo_ref, halves_ref, mine_ref, given_ref,
    next_ref, parts_ref, onorm_ref, right_ref, rot_ref, moved_ref, norms_ref, sems, out_sem
):

    for k in range(GROUPS):
        piece = (mine_ref, given_ref)[k // 4].at[pl.ds(GROUP * (k % 4), GROUP), pl.ds(0, PAIRW)]
        pltpu.make_async_copy(piece, rot_ref.at[pl.ds(GROUP * k, GROUP)], sems.at[1, k]).start()

    def fetch(g):
        for k in range(GROUP):
            q = GROUP * g + k
            i = tab_ref[q]
            for h in range(2):
                pltpu.make_async_copy(
                    halves_ref.at[order_ref[2 * i + h]], right_ref.at[q, :, h], sems.at[0, g]
                ).start()

    for g in range(GROUPS):
        fetch(g)
    core = place_ref[2]
    for half, norm_ref in ((core, normc_ref), (1 - core, normo_ref)):
        rows = pl.ds(pl.multiple_of(half * TILES, TILES), TILES)
        norms_ref[0, rows, :] = norm_ref[...]
        norms_ref[1, rows, :] = pltpu.roll(norm_ref[...], HALF, 1)

    def spot(quarter, j):
        mine = quarter ^ place_ref[j]
        return (mine & 1) * 2 + (mine >> 1)

    def group(g, carry):
        part = pl.ds(GROUP * g, GROUP)
        whole_copy(right_ref.at[part], sems.at[0, g]).wait()
        whole_copy(rot_ref.at[part], sems.at[1, g]).wait()
        todo = [GROUP * g + k for k in range(GROUP)]
        index = [tab_ref[q] for q in todo]
        lefts = []
        for q, i in zip(todo, index):
            bu, bl = order_ref[2 * i], order_ref[2 * i + 1]
            nu = norms_ref[bu % 2, pl.ds(bu // 2, 1), :]
            nl = norms_ref[1 - bl % 2, pl.ds(bl // 2, 1), :]
            scale = scales(jnp.where(lanes((1, PAIRW)) < HALF, nu, nl))
            lefts.append(left_operand(rot_ref[q] * scale))
        values = [
            split(product(left, right_ref[q].reshape(2 * PAIRW, SAMP)))
            for left, q in zip(lefts, todo)
        ]
        for i, pieces_of in zip(index, values):
            slots = next_slots(i)
            for part_of, value in enumerate(pieces_of):
                for h, slot in enumerate(slots):
                    moved_ref[slot // 2, part_of, slot % 2] = value[h * HALF : (h + 1) * HALF]
        for i, (high, low) in zip(index, values):
            gram = self_gram(jnp.concatenate([high, low], 0))
            onorm_ref[pl.ds(i, 1), :] = diagonal_row(gram)
            both = jnp.where(upper_or_diagonal(), gram[:HALF], pltpu.roll(gram[HALF:], HALF, 1))
            both = jnp.where(lanes((HALF, PAIRW)) < HALF, both, gram[:HALF])
            p, j = i // 2, i % 2
            parts_ref[spot(0, j), j, p] = both[0:24]
            parts_ref[spot(1, j), j, p] = both[24:48]
            parts_ref[spot(2, j), j, p, 0:16] = both[48:64]
        return carry

    lax.fori_loop(0, GROUPS, group, 0)

    copy = pltpu.make_async_copy(moved_ref, next_ref.at[pl.ds(0, NPAIR)], out_sem)
    copy.start()

    def cross(g, carry):
        wides = []
        for k in range(GROUP):
            upper = moved_ref[GROUP * g + k, :, 0].reshape(PAIRW, SAMP)
            lower = moved_ref[GROUP * g + k, :, 1].reshape(PAIRW, SAMP)
            wides.append(outer(upper, lower))
        for k, wide in enumerate(wides):
            folded = wide[:HALF] + wide[HALF:]
            folded = folded + pltpu.roll(folded, HALF, 1)
            packed = jnp.where(lanes((32, PAIRW)) < HALF, folded[:32], folded[32:])
            p, j = GROUP // 2 * g + k // 2, k % 2
            parts_ref[spot(2, j), j, p, 16:24] = packed[:8]
            parts_ref[spot(3, j), j, p] = packed[8:]
        return carry

    lax.fori_loop(0, GROUPS, cross, 0)
    copy.wait()


def step0(tab, order, place, normc, normo, halves, mine, given):
    smem = pl.BlockSpec(memory_space=pltpu.SMEM)
    vmem = pl.BlockSpec(memory_space=pltpu.VMEM)
    hbm = pl.BlockSpec(memory_space=pltpu.HBM)
    return pl.pallas_call(
        step0_kernel,
        in_specs=[smem] * 3 + [vmem] * 2 + [hbm] * 3,
        out_specs=[hbm, vmem, vmem],
        out_shape=[
            jax.ShapeDtypeStruct((ROOM * NPAIR,) + OPERAND[1:], BF16),
            jax.ShapeDtypeStruct((4, 2, NDEV, QUARTER, PAIRW), F32),
            jax.ShapeDtypeStruct((NPAIR, PAIRW), F32),
        ],
        scratch_shapes=[
            pltpu.VMEM(OPERAND, BF16),
            pltpu.VMEM((NPAIR, PAIRW, PAIRW), F32),
            pltpu.VMEM(OPERAND, BF16),
            pltpu.VMEM((2, NPAIR, PAIRW), F32),
            pltpu.SemaphoreType.DMA((2, GROUPS)),
            pltpu.SemaphoreType.DMA,
        ],
        compiler_params=pltpu.CompilerParams(vmem_limit_bytes=44 * MIB),
        cost_estimate=pl.CostEstimate(flops=MIB, bytes_accessed=MIB // 8, transcendentals=0),
        name="step0",
    )(tab, order, place, normc, normo, halves, mine, given)


def step1_kernel(
    norm_ref, operand_ref, rot_ref, parta_ref, partb_ref, pay_ref, right_ref, norms_ref, sems
):
    for g in range(GROUPS):
        part = pl.ds(GROUP * g, GROUP)
        pltpu.make_async_copy(operand_ref.at[part], right_ref.at[part], sems.at[g]).start()
    norms_ref[0] = norm_ref[...]
    norms_ref[1] = pltpu.roll(norm_ref[...], HALF, 1)
    pay_ref[:, 256:PAYROWS, :PAIRW] = parta_ref[...]
    pay_ref[:, 256:PAYROWS, PAIRW:] = partb_ref[...]

    def group(g, carry):
        whole_copy(right_ref.at[pl.ds(GROUP * g, GROUP)], sems.at[g]).wait()
        index = [GROUP * g + k for k in range(GROUP)]
        lefts = []
        for i in index:
            nu = norms_ref[jnp.where(i == 1, 1, 0), pl.ds(jnp.maximum(i - 1, 0), 1), :]
            nl = norms_ref[
                jnp.where(i == NPAIR - 1, 1, 0), pl.ds(jnp.minimum(i + 1, NPAIR - 1), 1), :
            ]
            scale = scales(jnp.where(lanes((1, PAIRW)) < HALF, nu, nl))
            lefts.append(left_operand(rot_ref[i] * scale))
        values = [
            product(left, right_ref[i].reshape(2 * PAIRW, SAMP)) for left, i in zip(lefts, index)
        ]
        for i, value in zip(index, values):
            for h, slot in enumerate(next_slots(i)):
                spot = pl.ds(pl.multiple_of((slot % 4) * HALF, HALF), HALF)
                pay_ref[slot // 4, spot, :] = value[h * HALF : (h + 1) * HALF]
        return carry

    lax.fori_loop(0, GROUPS, group, 0)


def step1(norm, operand, rot, parta, partb):
    vmem = pl.BlockSpec(memory_space=pltpu.VMEM)
    return pl.pallas_call(
        step1_kernel,
        in_specs=[vmem, pl.BlockSpec(memory_space=pltpu.HBM), vmem, vmem, vmem],
        out_specs=vmem,
        out_shape=jax.ShapeDtypeStruct((NDEV, PAYROWS, SAMP), F32),
        scratch_shapes=[
            pltpu.VMEM(OPERAND, BF16),
            pltpu.VMEM((2, NPAIR, PAIRW), F32),
            pltpu.SemaphoreType.DMA((GROUPS,)),
        ],
        compiler_params=pltpu.CompilerParams(vmem_limit_bytes=34 * MIB),
        cost_estimate=pl.CostEstimate(flops=3 << 30, bytes_accessed=24 * MIB, transcendentals=0),
        name="step1",
    )(norm, operand, rot, parta, partb)


CHUNK = 4
CHUNKS = NDEV // CHUNK


def parts_kernel(place_ref, y_ref, placed_ref):
    sums = []
    for z_odd in range(2):
        source = [s for s in range(NDEV) if (s // (2 * NX)) % 2 == z_odd]
        sums.append(sum(y_ref[s, 256:PAYROWS, :] for s in source))
    placed_ref[...] = jnp.zeros_like(placed_ref)
    row, core = place_ref[0], place_ref[2]
    spots = [pl.ds(pl.multiple_of(QUARTER * q, QUARTER), QUARTER) for q in (row, core, core + 2)]
    placed_ref[0, spots[0], :] = sums[0][:, :PAIRW] + sums[1][:, :PAIRW]
    placed_ref[1, spots[1], :] = sums[0][:, PAIRW:]
    placed_ref[1, spots[2], :] = sums[1][:, PAIRW:]


def parts(place, y):
    vmem = pl.BlockSpec(memory_space=pltpu.VMEM)
    return pl.pallas_call(
        parts_kernel,
        in_specs=[pl.BlockSpec(memory_space=pltpu.SMEM), vmem],
        out_specs=vmem,
        out_shape=jax.ShapeDtypeStruct((2, 4 * QUARTER, PAIRW), F32),
        compiler_params=pltpu.CompilerParams(vmem_limit_bytes=14 * MIB),
        cost_estimate=pl.CostEstimate(flops=MIB, bytes_accessed=MIB, transcendentals=0),
        name="parts",
    )(place, y)


def gram2_kernel(y_ref, norm_ref, gram_ref):
    totals = [None, None]
    for g in range(CHUNKS):
        source = range(CHUNK * g, CHUNK * (g + 1))
        for j in range(2):
            halves = [split(y_ref[s, j * PAIRW : (j + 1) * PAIRW, :]) for s in source]
            high = jnp.concatenate([h for h, _ in halves], 1)
            low = jnp.concatenate([l for _, l in halves], 1)
            term = outer(high, jnp.concatenate([high, low], 0))
            totals[j] = term if g == 0 else totals[j] + term
    both = []
    for j in range(2):
        mixed = totals[j][:, PAIRW:]
        gram = totals[j][:, :PAIRW] + mixed + mixed.T
        both.append(gram)
        norm_ref[j] = jnp.broadcast_to(diagonal_row(gram), (8, PAIRW))
    gram_ref[...] = jnp.where(upper_or_diagonal(PAIRW), both[0], both[1])


def gram2(y):
    vmem = pl.BlockSpec(memory_space=pltpu.VMEM)
    return pl.pallas_call(
        gram2_kernel,
        in_specs=[vmem],
        out_specs=[vmem, vmem],
        out_shape=[
            jax.ShapeDtypeStruct((2, 8, PAIRW), F32),
            jax.ShapeDtypeStruct((PAIRW, PAIRW), F32),
        ],
        compiler_params=pltpu.CompilerParams(vmem_limit_bytes=14 * MIB),
        cost_estimate=pl.CostEstimate(flops=2 << 30, bytes_accessed=10 * MIB, transcendentals=0),
        name="gram2",
    )(y)


def step2_kernel(norm_ref, rot_ref, y_ref, out_ref, turned_ref, out_sem):
    lefts = [left_operand(rot_ref[j] * scales(norm_ref[j, 0:1])) for j in range(2)]
    for g in range(CHUNKS):
        for j in range(2):
            here = slice(j * PAIRW, (j + 1) * PAIRW)
            for s in range(CHUNK * g, CHUNK * (g + 1)):
                right = jnp.concatenate(split(y_ref[s, here, :]), 0)
                turned_ref[here, s * SAMP : (s + 1) * SAMP] = product(lefts[j], right)
        part = pl.ds(CHUNK * SAMP * g, CHUNK * SAMP)
        pltpu.make_async_copy(turned_ref.at[:, part], out_ref.at[:, part], out_sem).start()
    whole_copy(turned_ref, out_sem).wait()


def step2(norm, rot, y):
    vmem = pl.BlockSpec(memory_space=pltpu.VMEM)
    return pl.pallas_call(
        step2_kernel,
        in_specs=[vmem, vmem, vmem],
        out_specs=pl.BlockSpec(memory_space=pl.ANY),
        out_shape=jax.ShapeDtypeStruct((256, NDEV * SAMP), F32),
        scratch_shapes=[pltpu.VMEM((2 * PAIRW, NDEV * SAMP), F32), pltpu.SemaphoreType.DMA],
        compiler_params=pltpu.CompilerParams(vmem_limit_bytes=24 * MIB),
        cost_estimate=pl.CostEstimate(flops=2 << 30, bytes_accessed=18 * MIB, transcendentals=0),
        name="step2",
    )(norm, rot, y)


def sandwich(mixing_t, gram):
    left = left_operand(mixing_t)
    inner = product(left, jnp.concatenate(split(gram), 0))
    turned = product(left, jnp.concatenate(split(inner.T), 0))
    return turned.T


def grams_kernel(place_ref, norm_ref, norm2_ref, rows_ref, rot1_ref, rot2_ref, out_ref):
    shape = (HALF, PAIRW)
    left = lanes(shape) < HALF
    zero = jnp.zeros(shape, F32)
    keeps = upper_or_diagonal()
    eye = lax.broadcasted_iota(jnp.int32, shape, 0) == lanes(shape)

    def turn(value):
        return pltpu.roll(value, HALF, 1)

    def blocks(both, norm_row):
        other = jnp.concatenate([jnp.where(left, both, zero), zero], 0).T[:HALF]
        lower = jnp.where(keeps, other, both)
        return jnp.where(keeps, both, other), jnp.where(eye, turn(norm_row), lower)

    def symmetric(upper, cross, lower):
        full = jnp.concatenate(
            [jnp.where(left, upper, cross), jnp.where(left, zero, turn(lower))], 0
        )
        low_left = (lanes((PAIRW, PAIRW)) < HALF) & (
            lax.broadcasted_iota(jnp.int32, (PAIRW, PAIRW), 0) >= HALF
        )
        return jnp.where(low_left, full.T, full)

    p = place_ref[5]
    first, last = place_ref[3] == 1, place_ref[4] == 1
    sums = [rows_ref[128:224], rows_ref[224:320]]
    square = rows_ref[:PAIRW]
    above_diagonal = upper_or_diagonal(PAIRW)
    on_diagonal = lax.broadcasted_iota(jnp.int32, square.shape, 0) == lanes(square.shape)
    step2_grams = [
        jnp.where(above_diagonal, square, square.T),
        jnp.where(on_diagonal, norm2_ref[1, 0:1], jnp.where(above_diagonal, square.T, square)),
    ]

    def norm_row(i):
        return norm_ref[pl.ds(i, 1), :]

    own = [blocks(sums[j][:HALF], norm_row(2 * p + j)) for j in range(2)]
    below = blocks(rows_ref[320:384], norm_row(2 * p))[0]
    above = blocks(rows_ref[384:448], norm_row(jnp.minimum(2 * p + 2, NPAIR - 1)))[1]
    uppers = [jnp.where(first, own[0][0], below), jnp.where(first, own[0][1], own[0][0])]
    lowers = [own[1][1], jnp.where(last, own[1][0], above)]
    for j in range(2):
        out_ref[0, j] = symmetric(own[j][0], sums[j][:HALF], own[j][1]) * (1.0 / ROWS)
        packed = sums[j][HALF:]
        gram = symmetric(uppers[j], jnp.concatenate([turn(packed), packed], 0), lowers[j])
        for t, rot, full in (
            (1, rot1_ref[j], gram), (2, rot2_ref[j], step2_grams[j])
        ):
            out_ref[t, j] = sandwich(rot * scales(diagonal_row(full)), full) * (1.0 / ROWS)


def grams(place, norm, norm2, rows, rot1, rot2):
    vmem = pl.BlockSpec(memory_space=pltpu.VMEM)
    return pl.pallas_call(
        grams_kernel,
        in_specs=[pl.BlockSpec(memory_space=pltpu.SMEM)] + [vmem] * 5,
        out_specs=vmem,
        out_shape=jax.ShapeDtypeStruct((3, 2, PAIRW, PAIRW), F32),
        compiler_params=pltpu.CompilerParams(vmem_limit_bytes=16 * MIB),
        cost_estimate=pl.CostEstimate(flops=1 << 20, bytes_accessed=2 * MIB, transcendentals=0),
        name="grams",
    )(place, norm, norm2, rows, rot1, rot2)


def body(samples_slab, block_order, rotations):
    pair, row = lax.axis_index("pair"), lax.axis_index("row")
    core = row % 2
    z_odd = (pair // (NX * 2)) % 2
    place = jnp.stack(
        [row, 2 * z_odd + core, core, pair == 0, pair == NDEV - 1, pair]
    ).astype(jnp.int32)
    even = 2 * jnp.arange(NDEV, dtype=jnp.int32)
    tab = jnp.concatenate([even + core, even + (1 - core)])
    x = samples_slab[0]
    norm0, give, own0, quarter1, turned = norms(place, x, rotations)
    rot1 = lax.all_gather(quarter1, BOTH, axis=0, tiled=True).reshape(NPAIR, PAIRW, PAIRW)
    copies = spread(own0, norm0, exchange(give, CORE))
    mine = lax.all_to_all(copies, "pair", 0, 0)
    halves = prepare(x)
    mine, halves = together(mine, halves)
    theirs = exchange(mine, CORE)
    norm0 = add_over(collect(mine), YLO)
    operand, given, norm1 = step0(
        tab, block_order, place, norm0, exchange(norm0, CORE), halves, mine, theirs
    )
    kept = given[:2] + exchange(given[2:], CORE)
    norm1 = add_over(norm1, Z1, YLO)
    kept, _ = together(kept, norm1)
    quarters = [kept[0, j] + exchange(kept[1, j], flip) for j, flip in enumerate((YLO, Z1))]
    norm1 = add_over(norm1, Z3, YBOTH, X1, X3, CORE)
    payload = step1(norm1, operand, rot1, *quarters)
    arrived = lax.all_to_all(payload, "pair", 0, 0)
    sums = parts(place, arrived)
    arrived, sums = together(arrived, sums)
    below = lax.ppermute(sums[1, :HALF], "pair", [(k, k + 1) for k in range(NDEV - 1)])
    above = lax.ppermute(sums[0, :HALF], "pair", [(k + 1, k) for k in range(NDEV - 1)])
    norm2, gram = gram2(arrived)
    norm2 = add_over(norm2, CORE)
    rows = [gram, sums.reshape(8 * QUARTER, PAIRW), below, above]
    rows = add_over(jnp.concatenate(rows, 0), CORE)
    norm2 = add_over(norm2, YLO)
    norm2, rows = together(norm2, rows)
    rows = add_over(rows, YLO)
    rotated = step2(norm2, turned[1], arrived)
    return rotated, grams(place, norm1, norm2, rows, turned[0], turned[1])


def solution(mesh):
    in_specs = (P("row", "pair", None), P(), P(None, "pair", None, None))
    out_specs = (P("pair", "row"), P(None, "pair", None, None))
    return jax.shard_map(body, mesh=mesh, in_specs=in_specs, out_specs=out_specs, check_vma=False)
```

```python
import functools
import itertools

import jax
import jax.numpy as jnp
from jax import lax
from jax.experimental import pallas as pl
from jax.experimental.pallas import tpu as pltpu
from jax.sharding import PartitionSpec as P


BOTH = ("pair", "row")
NZ, NX, NY, NC = 4, 4, 2, 2
NPAIR = 64
PAIRW = 128
HALF = 64
SAMP = 256
NDEV = 32
ROWS = 32768
EPS = 1e-06
QUARTER = 24
PAYROWS = 256 + QUARTER
MIB = 1 << 20
F32, BF16 = jnp.float32, jnp.bfloat16


def flat(z, x, yh, yl, c):
    return (((z * NX + x) * 2 + yh) * 2 + yl) * 2 + c


def exchange(value, flip):
    pairs = []
    for here in itertools.product(range(NZ), range(NX), range(2), range(2), range(2)):
        there = tuple(a ^ b for a, b in zip(here, flip))
        pairs.append((flat(*here), flat(*there)))
    return lax.ppermute(value, BOTH, pairs)


X1, X3, Z1, Z3 = (0, 1, 0, 0, 0), (0, 3, 0, 0, 0), (1, 0, 0, 0, 0), (3, 0, 0, 0, 0)
YLO, YBOTH, CORE = (0, 0, 0, 1, 0), (0, 0, 1, 1, 0), (0, 0, 0, 0, 1)


def add_over(value, *flips):
    for flip in flips:
        value = value + exchange(value, flip)
    return value


def together(*values):
    return lax.optimization_barrier(values)


def split(value):
    high = value.astype(BF16)
    return high, (value - high.astype(F32)).astype(BF16)


def left_operand(mixing_t):
    high, low = split(mixing_t)
    return jnp.concatenate(
        [
            jnp.concatenate([high, high], 1),
            jnp.concatenate([low, jnp.zeros_like(low)], 1),
        ],
        0,
    )


def product(left, right):
    wide = jnp.dot(left, right, preferred_element_type=F32)
    return wide[:PAIRW] + wide[PAIRW:]


def outer(a, b):
    return lax.dot_general(a, b, (((1,), (1,)), ((), ())), preferred_element_type=F32)


def self_gram(stacked):
    wide = outer(stacked, stacked)
    return wide[:PAIRW, :PAIRW] + wide[PAIRW:, :PAIRW] + wide[:PAIRW, PAIRW:]


def diagonal_row(gram):
    size = gram.shape[0]
    eye = lax.broadcasted_iota(jnp.int32, (size, size), 0) == lax.broadcasted_iota(
        jnp.int32, (size, size), 1
    )
    return jnp.sum(jnp.where(eye, gram, 0.0), axis=0, keepdims=True)


def scales(norm_row):
    return lax.rsqrt(norm_row / ROWS + EPS)


def lanes(shape):
    return lax.broadcasted_iota(jnp.int32, shape, 1)


def upper_or_diagonal(rows=HALF):
    shape = (rows, PAIRW)
    return lax.broadcasted_iota(jnp.int32, shape, 0) <= lanes(shape)


def next_slots(i):
    upper = jnp.where(i == 0, 0, jnp.where(i == NPAIR - 1, 2 * NPAIR - 1, 2 * i + 2))
    lower = jnp.where(i == 0, 2, 2 * i - 1)
    return upper, lower


TILES = NPAIR // 2


def norms_kernel(
    x_ref, rotations_ref, keep_ref, give_ref, own_ref, quarter_ref, turned_ref,
    held_ref, rot_ref, rows_ref, sems, rot_sem
):
    count = sems.shape[0]
    width = NPAIR // count

    def copy(g):
        part = pl.ds(g * width * PAIRW, width * PAIRW)
        return pltpu.make_async_copy(x_ref.at[:, part], held_ref.at[:, part], sems.at[g])

    rot_copy = pltpu.make_async_copy(rotations_ref, rot_ref, rot_sem)
    rot_copy.start()
    for g in range(count):
        copy(g).start()
    row = lax.axis_index("row")
    core = lax.rem(row, 2)
    rot_copy.wait()
    own_ref[...] = rot_ref[0, core].T
    for t in range(1, 3):
        for j in range(2):
            turned_ref[t - 1, j] = rot_ref[t, j].T
    half = pl.ds(pl.multiple_of(core * HALF, HALF), HALF)
    quarter_ref[...] = turned_ref[0, lax.div(row, 2), half, :]
    for g in range(count):
        copy(g).wait()
        for t in range(width * g, width * (g + 1)):
            tile = held_ref[:, t * PAIRW : (t + 1) * PAIRW]
            rows_ref[t // TILES, t % TILES : t % TILES + 1, :] = jnp.sum(
                tile * tile, axis=0, keepdims=True
            )
    keep_ref[...] = rows_ref[core]
    give_ref[...] = rows_ref[1 - core]


def norms(x, rotations):
    vmem = pl.BlockSpec(memory_space=pltpu.VMEM)
    hbm = pl.BlockSpec(memory_space=pltpu.HBM)
    return pl.pallas_call(
        norms_kernel,
        in_specs=[hbm, hbm],
        out_specs=[vmem] * 5,
        out_shape=[
            jax.ShapeDtypeStruct((TILES, PAIRW), F32),
            jax.ShapeDtypeStruct((TILES, PAIRW), F32),
            jax.ShapeDtypeStruct((PAIRW, PAIRW), F32),
            jax.ShapeDtypeStruct((HALF, PAIRW), F32),
            jax.ShapeDtypeStruct((2, 2, PAIRW, PAIRW), F32),
        ],
        scratch_shapes=[
            pltpu.VMEM((SAMP, NPAIR * PAIRW), F32),
            pltpu.VMEM((3, 2, PAIRW, PAIRW), F32),
            pltpu.VMEM((2, TILES, PAIRW), F32),
            pltpu.SemaphoreType.DMA((8,)),
            pltpu.SemaphoreType.DMA,
        ],
        compiler_params=pltpu.CompilerParams(vmem_limit_bytes=58 * MIB),
        cost_estimate=pl.CostEstimate(flops=8 * MIB, bytes_accessed=8 * MIB, transcendentals=0),
        name="norms",
    )(x, rotations)


def prepare_kernel(x_ref, halves_ref):
    tiles = x_ref.shape[1] // PAIRW
    for t in range(tiles):
        tile = x_ref[:, t * PAIRW : (t + 1) * PAIRW]
        high, low = split(tile.T)
        for h in range(2):
            halves_ref[2 * t + h, 0] = high[h * HALF : (h + 1) * HALF]
            halves_ref[2 * t + h, 1] = low[h * HALF : (h + 1) * HALF]


def prepare(x):
    width = 1024
    blocks = width // HALF
    return pl.pallas_call(
        prepare_kernel,
        grid=(x.shape[1] // width,),
        in_specs=[pl.BlockSpec((SAMP, width), lambda g: (0, g))],
        out_specs=pl.BlockSpec((blocks, 2, HALF, SAMP), lambda g: (g, 0, 0, 0)),
        out_shape=jax.ShapeDtypeStruct((2 * NPAIR, 2, HALF, SAMP), BF16),
        compiler_params=pltpu.CompilerParams(vmem_limit_bytes=58 * MIB),
        cost_estimate=pl.CostEstimate(flops=MIB, bytes_accessed=MIB // 8, transcendentals=0),
        name="prepare",
    )(x)


SENT = PAIRW + TILES


def spread_kernel(own_ref, norm_ref, given_ref, copies_ref):
    own = own_ref[...]
    norm = norm_ref[...] + given_ref[...]

    def copy(k, carry):
        copies_ref[k, :PAIRW] = own
        copies_ref[k, PAIRW:] = norm
        return carry

    lax.fori_loop(0, NDEV, copy, 0, unroll=4)


def spread(own, norm, given):
    vmem = pl.BlockSpec(memory_space=pltpu.VMEM)
    return pl.pallas_call(
        spread_kernel,
        in_specs=[vmem] * 3,
        out_specs=vmem,
        out_shape=jax.ShapeDtypeStruct((NDEV, SENT, PAIRW), F32),
        compiler_params=pltpu.CompilerParams(vmem_limit_bytes=58 * MIB),
        cost_estimate=pl.CostEstimate(flops=MIB, bytes_accessed=MIB // 8, transcendentals=0),
        name="spread",
    )(own, norm, given)


def collect_kernel(arrived_ref, norm_ref):
    norm_ref[...] = sum(arrived_ref[s, PAIRW:] for s in range(NDEV))


def collect(arrived):
    vmem = pl.BlockSpec(memory_space=pltpu.VMEM)
    return pl.pallas_call(
        collect_kernel,
        in_specs=[vmem],
        out_specs=vmem,
        out_shape=jax.ShapeDtypeStruct((TILES, PAIRW), F32),
        compiler_params=pltpu.CompilerParams(vmem_limit_bytes=8 * MIB),
        cost_estimate=pl.CostEstimate(flops=MIB, bytes_accessed=MIB // 8, transcendentals=0),
        name="collect",
    )(arrived)


GROUP = 8
GROUPS = NPAIR // GROUP
OPERAND = (NPAIR, 2, 2, HALF, SAMP)
ROOM = 4


def whole_copy(ref, sem):
    return pltpu.make_async_copy(ref, ref, sem)


def step0_kernel(
    tab_ref, order_ref, place_ref, normc_ref, normo_ref, halves_ref, mine_ref, given_ref,
    next_ref, parts_ref, onorm_ref, right_ref, rot_ref, moved_ref, norms_ref, sems, out_sem
):

    def fetch(q, carry):
        i = tab_ref[q]
        for h in range(2):
            pltpu.make_async_copy(
                halves_ref.at[order_ref[2 * i + h]], right_ref.at[q, :, h], sems.at[0, q // GROUP]
            ).start()
        return carry

    lax.fori_loop(0, NPAIR, fetch, 0)
    for k in range(GROUPS):
        piece = (mine_ref, given_ref)[k // 4].at[pl.ds(GROUP * (k % 4), GROUP), pl.ds(0, PAIRW)]
        pltpu.make_async_copy(piece, rot_ref.at[pl.ds(GROUP * k, GROUP)], sems.at[1, k]).start()

    core = place_ref[2]
    for half, norm_ref in ((core, normc_ref), (1 - core, normo_ref)):
        rows = pl.ds(pl.multiple_of(half * TILES, TILES), TILES)
        norms_ref[0, rows, :] = norm_ref[...]
        norms_ref[1, rows, :] = pltpu.roll(norm_ref[...], HALF, 1)

    def spot(quarter, j):
        mine = quarter ^ place_ref[j]
        return (mine & 1) * 2 + (mine >> 1)

    def group(g, carry):
        part = pl.ds(GROUP * g, GROUP)
        whole_copy(right_ref.at[part], sems.at[0, g]).wait()
        whole_copy(rot_ref.at[part], sems.at[1, g]).wait()
        todo = [GROUP * g + k for k in range(GROUP)]
        index = [tab_ref[q] for q in todo]
        lefts = []
        for q, i in zip(todo, index):
            bu, bl = order_ref[2 * i], order_ref[2 * i + 1]
            nu = norms_ref[bu % 2, pl.ds(bu // 2, 1), :]
            nl = norms_ref[1 - bl % 2, pl.ds(bl // 2, 1), :]
            scale = scales(jnp.where(lanes((1, PAIRW)) < HALF, nu, nl))
            lefts.append(left_operand(rot_ref[q] * scale))
        values = [
            split(product(left, right_ref[q].reshape(2 * PAIRW, SAMP)))
            for left, q in zip(lefts, todo)
        ]
        for i, pieces_of in zip(index, values):
            slots = next_slots(i)
            for part_of, value in enumerate(pieces_of):
                for h, slot in enumerate(slots):
                    moved_ref[slot // 2, part_of, slot % 2] = value[h * HALF : (h + 1) * HALF]
        for i, (high, low) in zip(index, values):
            gram = self_gram(jnp.concatenate([high, low], 0))
            onorm_ref[pl.ds(i, 1), :] = diagonal_row(gram)
            both = jnp.where(upper_or_diagonal(), gram[:HALF], pltpu.roll(gram[HALF:], HALF, 1))
            both = jnp.where(lanes((HALF, PAIRW)) < HALF, both, gram[:HALF])
            p, j = i // 2, i % 2
            parts_ref[spot(0, j), j, p] = both[0:24]
            parts_ref[spot(1, j), j, p] = both[24:48]
            parts_ref[spot(2, j), j, p, 0:16] = both[48:64]
        return carry

    lax.fori_loop(0, GROUPS, group, 0)

    copy = pltpu.make_async_copy(moved_ref, next_ref.at[pl.ds(0, NPAIR)], out_sem)
    copy.start()

    def cross(g, carry):
        wides = []
        for k in range(GROUP):
            upper = moved_ref[GROUP * g + k, :, 0].reshape(PAIRW, SAMP)
            lower = moved_ref[GROUP * g + k, :, 1].reshape(PAIRW, SAMP)
            wides.append(outer(upper, lower))
        for k, wide in enumerate(wides):
            folded = wide[:HALF] + wide[HALF:]
            folded = folded + pltpu.roll(folded, HALF, 1)
            packed = jnp.where(lanes((32, PAIRW)) < HALF, folded[:32], folded[32:])
            p, j = GROUP // 2 * g + k // 2, k % 2
            parts_ref[spot(2, j), j, p, 16:24] = packed[:8]
            parts_ref[spot(3, j), j, p] = packed[8:]
        return carry

    lax.fori_loop(0, GROUPS, cross, 0)
    copy.wait()


def step0(tab, order, place, normc, normo, halves, mine, given):
    smem = pl.BlockSpec(memory_space=pltpu.SMEM)
    vmem = pl.BlockSpec(memory_space=pltpu.VMEM)
    hbm = pl.BlockSpec(memory_space=pltpu.HBM)
    return pl.pallas_call(
        step0_kernel,
        in_specs=[smem] * 3 + [vmem] * 2 + [hbm] * 3,
        out_specs=[hbm, vmem, vmem],
        out_shape=[
            jax.ShapeDtypeStruct((ROOM * NPAIR,) + OPERAND[1:], BF16),
            jax.ShapeDtypeStruct((4, 2, NDEV, QUARTER, PAIRW), F32),
            jax.ShapeDtypeStruct((NPAIR, PAIRW), F32),
        ],
        scratch_shapes=[
            pltpu.VMEM(OPERAND, BF16),
            pltpu.VMEM((NPAIR, PAIRW, PAIRW), F32),
            pltpu.VMEM(OPERAND, BF16),
            pltpu.VMEM((2, NPAIR, PAIRW), F32),
            pltpu.SemaphoreType.DMA((2, GROUPS)),
            pltpu.SemaphoreType.DMA,
        ],
        compiler_params=pltpu.CompilerParams(vmem_limit_bytes=44 * MIB),
        cost_estimate=pl.CostEstimate(flops=MIB, bytes_accessed=MIB // 8, transcendentals=0),
        name="step0",
    )(tab, order, place, normc, normo, halves, mine, given)


def step1_kernel(
    norm_ref, operand_ref, rot_ref, parta_ref, partb_ref, pay_ref, right_ref, norms_ref, sems
):
    for g in range(GROUPS):
        part = pl.ds(GROUP * g, GROUP)
        pltpu.make_async_copy(operand_ref.at[part], right_ref.at[part], sems.at[g]).start()
    norms_ref[0] = norm_ref[...]
    norms_ref[1] = pltpu.roll(norm_ref[...], HALF, 1)
    pay_ref[:, 256:PAYROWS, :PAIRW] = parta_ref[...]
    pay_ref[:, 256:PAYROWS, PAIRW:] = partb_ref[...]

    def group(g, carry):
        whole_copy(right_ref.at[pl.ds(GROUP * g, GROUP)], sems.at[g]).wait()
        index = [GROUP * g + k for k in range(GROUP)]
        lefts = []
        for i in index:
            nu = norms_ref[jnp.where(i == 1, 1, 0), pl.ds(jnp.maximum(i - 1, 0), 1), :]
            nl = norms_ref[
                jnp.where(i == NPAIR - 1, 1, 0), pl.ds(jnp.minimum(i + 1, NPAIR - 1), 1), :
            ]
            scale = scales(jnp.where(lanes((1, PAIRW)) < HALF, nu, nl))
            lefts.append(left_operand(rot_ref[i] * scale))
        values = [
            product(left, right_ref[i].reshape(2 * PAIRW, SAMP)) for left, i in zip(lefts, index)
        ]
        for i, value in zip(index, values):
            for h, slot in enumerate(next_slots(i)):
                spot = pl.ds(pl.multiple_of((slot % 4) * HALF, HALF), HALF)
                pay_ref[slot // 4, spot, :] = value[h * HALF : (h + 1) * HALF]
        return carry

    lax.fori_loop(0, GROUPS, group, 0)


def step1(norm, operand, rot, parta, partb):
    vmem = pl.BlockSpec(memory_space=pltpu.VMEM)
    return pl.pallas_call(
        step1_kernel,
        in_specs=[vmem, pl.BlockSpec(memory_space=pltpu.HBM), vmem, vmem, vmem],
        out_specs=vmem,
        out_shape=jax.ShapeDtypeStruct((NDEV, PAYROWS, SAMP), F32),
        scratch_shapes=[
            pltpu.VMEM(OPERAND, BF16),
            pltpu.VMEM((2, NPAIR, PAIRW), F32),
            pltpu.SemaphoreType.DMA((GROUPS,)),
        ],
        compiler_params=pltpu.CompilerParams(vmem_limit_bytes=34 * MIB),
        cost_estimate=pl.CostEstimate(flops=3 << 30, bytes_accessed=24 * MIB, transcendentals=0),
        name="step1",
    )(norm, operand, rot, parta, partb)


CHUNK = 4
CHUNKS = NDEV // CHUNK


def parts_kernel(place_ref, y_ref, placed_ref):
    sums = []
    for z_odd in range(2):
        source = [s for s in range(NDEV) if (s // (2 * NX)) % 2 == z_odd]
        sums.append(sum(y_ref[s, 256:PAYROWS, :] for s in source))
    placed_ref[...] = jnp.zeros_like(placed_ref)
    row, core = place_ref[0], place_ref[2]
    spots = [pl.ds(pl.multiple_of(QUARTER * q, QUARTER), QUARTER) for q in (row, core, core + 2)]
    placed_ref[0, spots[0], :] = sums[0][:, :PAIRW] + sums[1][:, :PAIRW]
    placed_ref[1, spots[1], :] = sums[0][:, PAIRW:]
    placed_ref[1, spots[2], :] = sums[1][:, PAIRW:]


def parts(place, y):
    vmem = pl.BlockSpec(memory_space=pltpu.VMEM)
    return pl.pallas_call(
        parts_kernel,
        in_specs=[pl.BlockSpec(memory_space=pltpu.SMEM), vmem],
        out_specs=vmem,
        out_shape=jax.ShapeDtypeStruct((2, 4 * QUARTER, PAIRW), F32),
        compiler_params=pltpu.CompilerParams(vmem_limit_bytes=14 * MIB),
        cost_estimate=pl.CostEstimate(flops=MIB, bytes_accessed=MIB, transcendentals=0),
        name="parts",
    )(place, y)


def gram2_kernel(y_ref, norm_ref, gram_ref):
    totals = [None, None]
    for g in range(CHUNKS):
        source = range(CHUNK * g, CHUNK * (g + 1))
        for j in range(2):
            halves = [split(y_ref[s, j * PAIRW : (j + 1) * PAIRW, :]) for s in source]
            high = jnp.concatenate([h for h, _ in halves], 1)
            low = jnp.concatenate([l for _, l in halves], 1)
            term = outer(high, jnp.concatenate([high, low], 0))
            totals[j] = term if g == 0 else totals[j] + term
    both = []
    for j in range(2):
        mixed = totals[j][:, PAIRW:]
        gram = totals[j][:, :PAIRW] + mixed + mixed.T
        both.append(gram)
        norm_ref[j] = jnp.broadcast_to(diagonal_row(gram), (8, PAIRW))
    gram_ref[...] = jnp.where(upper_or_diagonal(PAIRW), both[0], both[1])


def gram2(y):
    vmem = pl.BlockSpec(memory_space=pltpu.VMEM)
    return pl.pallas_call(
        gram2_kernel,
        in_specs=[vmem],
        out_specs=[vmem, vmem],
        out_shape=[
            jax.ShapeDtypeStruct((2, 8, PAIRW), F32),
            jax.ShapeDtypeStruct((PAIRW, PAIRW), F32),
        ],
        compiler_params=pltpu.CompilerParams(vmem_limit_bytes=14 * MIB),
        cost_estimate=pl.CostEstimate(flops=2 << 30, bytes_accessed=10 * MIB, transcendentals=0),
        name="gram2",
    )(y)


def step2_kernel(norm_ref, rot_ref, y_ref, out_ref, turned_ref, out_sem):
    lefts = [left_operand(rot_ref[j] * scales(norm_ref[j, 0:1])) for j in range(2)]
    for g in range(CHUNKS):
        for j in range(2):
            here = slice(j * PAIRW, (j + 1) * PAIRW)
            for s in range(CHUNK * g, CHUNK * (g + 1)):
                right = jnp.concatenate(split(y_ref[s, here, :]), 0)
                turned_ref[here, s * SAMP : (s + 1) * SAMP] = product(lefts[j], right)
        part = pl.ds(CHUNK * SAMP * g, CHUNK * SAMP)
        pltpu.make_async_copy(turned_ref.at[:, part], out_ref.at[:, part], out_sem).start()
    whole_copy(turned_ref, out_sem).wait()


def step2(norm, rot, y):
    vmem = pl.BlockSpec(memory_space=pltpu.VMEM)
    return pl.pallas_call(
        step2_kernel,
        in_specs=[vmem, vmem, vmem],
        out_specs=pl.BlockSpec(memory_space=pl.ANY),
        out_shape=jax.ShapeDtypeStruct((256, NDEV * SAMP), F32),
        scratch_shapes=[pltpu.VMEM((2 * PAIRW, NDEV * SAMP), F32), pltpu.SemaphoreType.DMA],
        compiler_params=pltpu.CompilerParams(vmem_limit_bytes=24 * MIB),
        cost_estimate=pl.CostEstimate(flops=2 << 30, bytes_accessed=18 * MIB, transcendentals=0),
        name="step2",
    )(norm, rot, y)


def sandwich(mixing_t, gram):
    left = left_operand(mixing_t)
    inner = product(left, jnp.concatenate(split(gram), 0))
    turned = product(left, jnp.concatenate(split(inner.T), 0))
    return turned.T


def grams_kernel(place_ref, norm_ref, norm2_ref, rows_ref, rot1_ref, rot2_ref, out_ref):
    shape = (HALF, PAIRW)
    left = lanes(shape) < HALF
    zero = jnp.zeros(shape, F32)
    keeps = upper_or_diagonal()
    eye = lax.broadcasted_iota(jnp.int32, shape, 0) == lanes(shape)

    def turn(value):
        return pltpu.roll(value, HALF, 1)

    def blocks(both, norm_row):
        other = jnp.concatenate([jnp.where(left, both, zero), zero], 0).T[:HALF]
        lower = jnp.where(keeps, other, both)
        return jnp.where(keeps, both, other), jnp.where(eye, turn(norm_row), lower)

    def symmetric(upper, cross, lower):
        full = jnp.concatenate(
            [jnp.where(left, upper, cross), jnp.where(left, zero, turn(lower))], 0
        )
        low_left = (lanes((PAIRW, PAIRW)) < HALF) & (
            lax.broadcasted_iota(jnp.int32, (PAIRW, PAIRW), 0) >= HALF
        )
        return jnp.where(low_left, full.T, full)

    p = place_ref[5]
    first, last = place_ref[3] == 1, place_ref[4] == 1
    sums = [rows_ref[128:224], rows_ref[224:320]]
    square = rows_ref[:PAIRW]
    above_diagonal = upper_or_diagonal(PAIRW)
    on_diagonal = lax.broadcasted_iota(jnp.int32, square.shape, 0) == lanes(square.shape)
    step2_grams = [
        jnp.where(above_diagonal, square, square.T),
        jnp.where(on_diagonal, norm2_ref[1, 0:1], jnp.where(above_diagonal, square.T, square)),
    ]

    def norm_row(i):
        return norm_ref[pl.ds(i, 1), :]

    own = [blocks(sums[j][:HALF], norm_row(2 * p + j)) for j in range(2)]
    below = blocks(rows_ref[320:384], norm_row(2 * p))[0]
    above = blocks(rows_ref[384:448], norm_row(jnp.minimum(2 * p + 2, NPAIR - 1)))[1]
    uppers = [jnp.where(first, own[0][0], below), jnp.where(first, own[0][1], own[0][0])]
    lowers = [own[1][1], jnp.where(last, own[1][0], above)]
    for j in range(2):
        out_ref[0, j] = symmetric(own[j][0], sums[j][:HALF], own[j][1]) * (1.0 / ROWS)
        packed = sums[j][HALF:]
        gram = symmetric(uppers[j], jnp.concatenate([turn(packed), packed], 0), lowers[j])
        for t, rot, full in (
            (1, rot1_ref[j], gram), (2, rot2_ref[j], step2_grams[j])
        ):
            out_ref[t, j] = sandwich(rot * scales(diagonal_row(full)), full) * (1.0 / ROWS)


def grams(place, norm, norm2, rows, rot1, rot2):
    vmem = pl.BlockSpec(memory_space=pltpu.VMEM)
    return pl.pallas_call(
        grams_kernel,
        in_specs=[pl.BlockSpec(memory_space=pltpu.SMEM)] + [vmem] * 5,
        out_specs=vmem,
        out_shape=jax.ShapeDtypeStruct((3, 2, PAIRW, PAIRW), F32),
        compiler_params=pltpu.CompilerParams(vmem_limit_bytes=16 * MIB),
        cost_estimate=pl.CostEstimate(flops=1 << 20, bytes_accessed=2 * MIB, transcendentals=0),
        name="grams",
    )(place, norm, norm2, rows, rot1, rot2)


def body(samples_slab, block_order, rotations):
    pair, row = lax.axis_index("pair"), lax.axis_index("row")
    core = row % 2
    z_odd = (pair // (NX * 2)) % 2
    place = jnp.stack(
        [row, 2 * z_odd + core, core, pair == 0, pair == NDEV - 1, pair]
    ).astype(jnp.int32)
    even = 2 * jnp.arange(NDEV, dtype=jnp.int32)
    tab = jnp.concatenate([even + core, even + (1 - core)])
    x = samples_slab[0]
    norm0, give, own0, quarter1, turned = norms(x, rotations)
    rot1 = lax.all_gather(quarter1, BOTH, axis=0, tiled=True).reshape(NPAIR, PAIRW, PAIRW)
    copies = spread(own0, norm0, exchange(give, CORE))
    mine = lax.all_to_all(copies, "pair", 0, 0)
    halves = prepare(x)
    mine, halves = together(mine, halves)
    theirs = exchange(mine, CORE)
    norm0 = add_over(collect(mine), YLO)
    operand, given, norm1 = step0(
        tab, block_order, place, norm0, exchange(norm0, CORE), halves, mine, theirs
    )
    kept = given[:2] + exchange(given[2:], CORE)
    norm1 = add_over(norm1, Z1, YLO)
    kept, _ = together(kept, norm1)
    quarters = [kept[0, j] + exchange(kept[1, j], flip) for j, flip in enumerate((YLO, Z1))]
    norm1 = add_over(norm1, CORE, Z3, YBOTH, X1, X3)
    payload = step1(norm1, operand, rot1, *quarters)
    arrived = lax.all_to_all(payload, "pair", 0, 0)
    sums = parts(place, arrived)
    arrived, sums = together(arrived, sums)
    below = lax.ppermute(sums[1, :HALF], "pair", [(k, k + 1) for k in range(NDEV - 1)])
    above = lax.ppermute(sums[0, :HALF], "pair", [(k + 1, k) for k in range(NDEV - 1)])
    norm2, gram = gram2(arrived)
    norm2 = add_over(norm2, CORE)
    rows = [gram, sums.reshape(8 * QUARTER, PAIRW), below, above]
    rows = add_over(jnp.concatenate(rows, 0), CORE)
    norm2 = add_over(norm2, YLO)
    norm2, rows = together(norm2, rows)
    rows = add_over(rows, YLO)
    rotated = step2(norm2, turned[1], arrived)
    return rotated, grams(place, norm1, norm2, rows, turned[0], turned[1])


def solution(mesh):
    in_specs = (P("row", "pair", None), P(), P(None, "pair", None, None))
    out_specs = (P("pair", "row"), P(None, "pair", None, None))
    return jax.shard_map(body, mesh=mesh, in_specs=in_specs, out_specs=out_specs, check_vma=False)
```

```python
import functools
import itertools

import jax
import jax.numpy as jnp
from jax import lax
from jax.experimental import pallas as pl
from jax.experimental.pallas import tpu as pltpu
from jax.sharding import PartitionSpec as P


BOTH = ("pair", "row")
NZ, NX, NY, NC = 4, 4, 2, 2
NPAIR = 64
PAIRW = 128
HALF = 64
SAMP = 256
NDEV = 32
ROWS = 32768
EPS = 1e-06
QUARTER = 24
PAYROWS = 256 + QUARTER
MIB = 1 << 20
F32, BF16 = jnp.float32, jnp.bfloat16


def flat(z, x, yh, yl, c):
    return (((z * NX + x) * 2 + yh) * 2 + yl) * 2 + c


def exchange(value, flip):
    pairs = []
    for here in itertools.product(range(NZ), range(NX), range(2), range(2), range(2)):
        there = tuple(a ^ b for a, b in zip(here, flip))
        pairs.append((flat(*here), flat(*there)))
    return lax.ppermute(value, BOTH, pairs)


X1, X3, Z1, Z3 = (0, 1, 0, 0, 0), (0, 3, 0, 0, 0), (1, 0, 0, 0, 0), (3, 0, 0, 0, 0)
YLO, YBOTH, CORE = (0, 0, 0, 1, 0), (0, 0, 1, 1, 0), (0, 0, 0, 0, 1)


def add_over(value, *flips):
    for flip in flips:
        value = value + exchange(value, flip)
    return value


def together(*values):
    return lax.optimization_barrier(values)


def split(value):
    high = value.astype(BF16)
    return high, (value - high.astype(F32)).astype(BF16)


def left_operand(mixing_t):
    high, low = split(mixing_t)
    return jnp.concatenate(
        [
            jnp.concatenate([high, high], 1),
            jnp.concatenate([low, jnp.zeros_like(low)], 1),
        ],
        0,
    )


def product(left, right):
    wide = jnp.dot(left, right, preferred_element_type=F32)
    return wide[:PAIRW] + wide[PAIRW:]


def outer(a, b):
    return lax.dot_general(a, b, (((1,), (1,)), ((), ())), preferred_element_type=F32)


def self_gram(stacked):
    wide = outer(stacked, stacked)
    return wide[:PAIRW, :PAIRW] + wide[PAIRW:, :PAIRW] + wide[:PAIRW, PAIRW:]


def diagonal_row(gram):
    size = gram.shape[0]
    eye = lax.broadcasted_iota(jnp.int32, (size, size), 0) == lax.broadcasted_iota(
        jnp.int32, (size, size), 1
    )
    return jnp.sum(jnp.where(eye, gram, 0.0), axis=0, keepdims=True)


def scales(norm_row):
    return lax.rsqrt(norm_row / ROWS + EPS)


def lanes(shape):
    return lax.broadcasted_iota(jnp.int32, shape, 1)


def upper_or_diagonal(rows=HALF):
    shape = (rows, PAIRW)
    return lax.broadcasted_iota(jnp.int32, shape, 0) <= lanes(shape)


def next_slots(i):
    upper = jnp.where(i == 0, 0, jnp.where(i == NPAIR - 1, 2 * NPAIR - 1, 2 * i + 2))
    lower = jnp.where(i == 0, 2, 2 * i - 1)
    return upper, lower


TILES = NPAIR // 2


def norms_kernel(
    x_ref, rotations_ref, keep_ref, give_ref, own_ref, quarter_ref, turned_ref,
    held_ref, rot_ref, rows_ref, sems, rot_sem
):
    count = sems.shape[0]
    width = NPAIR // count

    def copy(g):
        part = pl.ds(g * width * PAIRW, width * PAIRW)
        return pltpu.make_async_copy(x_ref.at[:, part], held_ref.at[:, part], sems.at[g])

    rot_copy = pltpu.make_async_copy(rotations_ref, rot_ref, rot_sem)
    rot_copy.start()
    for g in range(count):
        copy(g).start()
    row = lax.axis_index("row")
    core = lax.rem(row, 2)
    rot_copy.wait()
    own_ref[...] = rot_ref[0, core].T
    for t in range(1, 3):
        for j in range(2):
            turned_ref[t - 1, j] = rot_ref[t, j].T
    half = pl.ds(pl.multiple_of(core * HALF, HALF), HALF)
    quarter_ref[...] = turned_ref[0, lax.div(row, 2), half, :]
    for g in range(count):
        copy(g).wait()
        for t in range(width * g, width * (g + 1)):
            tile = held_ref[:, t * PAIRW : (t + 1) * PAIRW]
            rows_ref[t // TILES, t % TILES : t % TILES + 1, :] = jnp.sum(
                tile * tile, axis=0, keepdims=True
            )
    keep_ref[...] = rows_ref[core]
    give_ref[...] = rows_ref[1 - core]


def norms(x, rotations):
    vmem = pl.BlockSpec(memory_space=pltpu.VMEM)
    hbm = pl.BlockSpec(memory_space=pltpu.HBM)
    return pl.pallas_call(
        norms_kernel,
        in_specs=[hbm, hbm],
        out_specs=[vmem] * 5,
        out_shape=[
            jax.ShapeDtypeStruct((TILES, PAIRW), F32),
            jax.ShapeDtypeStruct((TILES, PAIRW), F32),
            jax.ShapeDtypeStruct((PAIRW, PAIRW), F32),
            jax.ShapeDtypeStruct((HALF, PAIRW), F32),
            jax.ShapeDtypeStruct((2, 2, PAIRW, PAIRW), F32),
        ],
        scratch_shapes=[
            pltpu.VMEM((SAMP, NPAIR * PAIRW), F32),
            pltpu.VMEM((3, 2, PAIRW, PAIRW), F32),
            pltpu.VMEM((2, TILES, PAIRW), F32),
            pltpu.SemaphoreType.DMA((8,)),
            pltpu.SemaphoreType.DMA,
        ],
        compiler_params=pltpu.CompilerParams(vmem_limit_bytes=58 * MIB),
        cost_estimate=pl.CostEstimate(flops=8 * MIB, bytes_accessed=8 * MIB, transcendentals=0),
        name="norms",
    )(x, rotations)


def prepare_kernel(x_ref, halves_ref):
    tiles = x_ref.shape[1] // PAIRW
    for t in range(tiles):
        tile = x_ref[:, t * PAIRW : (t + 1) * PAIRW]
        high, low = split(tile.T)
        for h in range(2):
            halves_ref[2 * t + h, 0] = high[h * HALF : (h + 1) * HALF]
            halves_ref[2 * t + h, 1] = low[h * HALF : (h + 1) * HALF]


def prepare(x):
    width = 1024
    blocks = width // HALF
    return pl.pallas_call(
        prepare_kernel,
        grid=(x.shape[1] // width,),
        in_specs=[pl.BlockSpec((SAMP, width), lambda g: (0, g))],
        out_specs=pl.BlockSpec((blocks, 2, HALF, SAMP), lambda g: (g, 0, 0, 0)),
        out_shape=jax.ShapeDtypeStruct((2 * NPAIR, 2, HALF, SAMP), BF16),
        compiler_params=pltpu.CompilerParams(vmem_limit_bytes=58 * MIB),
        cost_estimate=pl.CostEstimate(flops=MIB, bytes_accessed=MIB // 8, transcendentals=0),
        name="prepare",
    )(x)


SENT = PAIRW + TILES


def spread_kernel(own_ref, norm_ref, given_ref, copies_ref):
    own = own_ref[...]
    norm = norm_ref[...] + given_ref[...]

    def copy(k, carry):
        copies_ref[k, :PAIRW] = own
        copies_ref[k, PAIRW:] = norm
        return carry

    lax.fori_loop(0, NDEV, copy, 0, unroll=4)


def spread(own, norm, given):
    vmem = pl.BlockSpec(memory_space=pltpu.VMEM)
    return pl.pallas_call(
        spread_kernel,
        in_specs=[vmem] * 3,
        out_specs=vmem,
        out_shape=jax.ShapeDtypeStruct((NDEV, SENT, PAIRW), F32),
        compiler_params=pltpu.CompilerParams(vmem_limit_bytes=58 * MIB),
        cost_estimate=pl.CostEstimate(flops=MIB, bytes_accessed=MIB // 8, transcendentals=0),
        name="spread",
    )(own, norm, given)


def collect_kernel(arrived_ref, norm_ref):
    norm_ref[...] = sum(arrived_ref[s, PAIRW:] for s in range(NDEV))


def collect(arrived):
    vmem = pl.BlockSpec(memory_space=pltpu.VMEM)
    return pl.pallas_call(
        collect_kernel,
        in_specs=[vmem],
        out_specs=vmem,
        out_shape=jax.ShapeDtypeStruct((TILES, PAIRW), F32),
        compiler_params=pltpu.CompilerParams(vmem_limit_bytes=8 * MIB),
        cost_estimate=pl.CostEstimate(flops=MIB, bytes_accessed=MIB // 8, transcendentals=0),
        name="collect",
    )(arrived)


GROUP = 16
GROUPS = NPAIR // GROUP
OPERAND = (NPAIR, 2, 2, HALF, SAMP)
ROOM = 4


def whole_copy(ref, sem):
    return pltpu.make_async_copy(ref, ref, sem)


def step0_kernel(
    tab_ref, order_ref, place_ref, normc_ref, normo_ref, halves_ref, mine_ref, given_ref,
    next_ref, parts_ref, onorm_ref, right_ref, rot_ref, moved_ref, norms_ref, sems, out_sem
):

    def fetch(q, carry):
        i = tab_ref[q]
        for h in range(2):
            pltpu.make_async_copy(
                halves_ref.at[order_ref[2 * i + h]], right_ref.at[q, :, h], sems.at[0, q // GROUP]
            ).start()
        return carry

    lax.fori_loop(0, NPAIR, fetch, 0)
    for k in range(GROUPS):
        source, first = divmod(GROUP * k, NDEV)
        piece = (mine_ref, given_ref)[source].at[pl.ds(first, GROUP), pl.ds(0, PAIRW)]
        pltpu.make_async_copy(piece, rot_ref.at[pl.ds(GROUP * k, GROUP)], sems.at[1, k]).start()

    core = place_ref[2]
    for half, norm_ref in ((core, normc_ref), (1 - core, normo_ref)):
        rows = pl.ds(pl.multiple_of(half * TILES, TILES), TILES)
        norms_ref[0, rows, :] = norm_ref[...]
        norms_ref[1, rows, :] = pltpu.roll(norm_ref[...], HALF, 1)

    def spot(quarter, j):
        mine = quarter ^ place_ref[j]
        return (mine & 1) * 2 + (mine >> 1)

    def group(g, carry):
        part = pl.ds(GROUP * g, GROUP)
        whole_copy(right_ref.at[part], sems.at[0, g]).wait()
        whole_copy(rot_ref.at[part], sems.at[1, g]).wait()
        todo = [GROUP * g + k for k in range(GROUP)]
        index = [tab_ref[q] for q in todo]
        lefts = []
        for q, i in zip(todo, index):
            bu, bl = order_ref[2 * i], order_ref[2 * i + 1]
            nu = norms_ref[bu % 2, pl.ds(bu // 2, 1), :]
            nl = norms_ref[1 - bl % 2, pl.ds(bl // 2, 1), :]
            scale = scales(jnp.where(lanes((1, PAIRW)) < HALF, nu, nl))
            lefts.append(left_operand(rot_ref[q] * scale))
        values = [
            split(product(left, right_ref[q].reshape(2 * PAIRW, SAMP)))
            for left, q in zip(lefts, todo)
        ]
        for i, pieces_of in zip(index, values):
            slots = next_slots(i)
            for part_of, value in enumerate(pieces_of):
                for h, slot in enumerate(slots):
                    moved_ref[slot // 2, part_of, slot % 2] = value[h * HALF : (h + 1) * HALF]
        for i, (high, low) in zip(index, values):
            gram = self_gram(jnp.concatenate([high, low], 0))
            onorm_ref[pl.ds(i, 1), :] = diagonal_row(gram)
            both = jnp.where(upper_or_diagonal(), gram[:HALF], pltpu.roll(gram[HALF:], HALF, 1))
            both = jnp.where(lanes((HALF, PAIRW)) < HALF, both, gram[:HALF])
            p, j = i // 2, i % 2
            parts_ref[spot(0, j), j, p] = both[0:24]
            parts_ref[spot(1, j), j, p] = both[24:48]
            parts_ref[spot(2, j), j, p, 0:16] = both[48:64]
        return carry

    lax.fori_loop(0, GROUPS, group, 0)

    copy = pltpu.make_async_copy(moved_ref, next_ref.at[pl.ds(0, NPAIR)], out_sem)
    copy.start()

    def cross(g, carry):
        wides = []
        for k in range(GROUP):
            upper = moved_ref[GROUP * g + k, :, 0].reshape(PAIRW, SAMP)
            lower = moved_ref[GROUP * g + k, :, 1].reshape(PAIRW, SAMP)
            wides.append(outer(upper, lower))
        for k, wide in enumerate(wides):
            folded = wide[:HALF] + wide[HALF:]
            folded = folded + pltpu.roll(folded, HALF, 1)
            packed = jnp.where(lanes((32, PAIRW)) < HALF, folded[:32], folded[32:])
            p, j = GROUP // 2 * g + k // 2, k % 2
            parts_ref[spot(2, j), j, p, 16:24] = packed[:8]
            parts_ref[spot(3, j), j, p] = packed[8:]
        return carry

    lax.fori_loop(0, GROUPS, cross, 0)
    copy.wait()


def step0(tab, order, place, normc, normo, halves, mine, given):
    smem = pl.BlockSpec(memory_space=pltpu.SMEM)
    vmem = pl.BlockSpec(memory_space=pltpu.VMEM)
    hbm = pl.BlockSpec(memory_space=pltpu.HBM)
    return pl.pallas_call(
        step0_kernel,
        in_specs=[smem] * 3 + [vmem] * 2 + [hbm] * 3,
        out_specs=[hbm, vmem, vmem],
        out_shape=[
            jax.ShapeDtypeStruct((ROOM * NPAIR,) + OPERAND[1:], BF16),
            jax.ShapeDtypeStruct((4, 2, NDEV, QUARTER, PAIRW), F32),
            jax.ShapeDtypeStruct((NPAIR, PAIRW), F32),
        ],
        scratch_shapes=[
            pltpu.VMEM(OPERAND, BF16),
            pltpu.VMEM((NPAIR, PAIRW, PAIRW), F32),
            pltpu.VMEM(OPERAND, BF16),
            pltpu.VMEM((2, NPAIR, PAIRW), F32),
            pltpu.SemaphoreType.DMA((2, GROUPS)),
            pltpu.SemaphoreType.DMA,
        ],
        compiler_params=pltpu.CompilerParams(vmem_limit_bytes=44 * MIB),
        cost_estimate=pl.CostEstimate(flops=MIB, bytes_accessed=MIB // 8, transcendentals=0),
        name="step0",
    )(tab, order, place, normc, normo, halves, mine, given)


def step1_kernel(
    norm_ref, operand_ref, rot_ref, parta_ref, partb_ref, pay_ref, right_ref, norms_ref, sems
):
    for g in range(GROUPS):
        part = pl.ds(GROUP * g, GROUP)
        pltpu.make_async_copy(operand_ref.at[part], right_ref.at[part], sems.at[g]).start()
    norms_ref[0] = norm_ref[...]
    norms_ref[1] = pltpu.roll(norm_ref[...], HALF, 1)
    pay_ref[:, 256:PAYROWS, :PAIRW] = parta_ref[...]
    pay_ref[:, 256:PAYROWS, PAIRW:] = partb_ref[...]

    def group(g, carry):
        whole_copy(right_ref.at[pl.ds(GROUP * g, GROUP)], sems.at[g]).wait()
        index = [GROUP * g + k for k in range(GROUP)]
        lefts = []
        for i in index:
            nu = norms_ref[jnp.where(i == 1, 1, 0), pl.ds(jnp.maximum(i - 1, 0), 1), :]
            nl = norms_ref[
                jnp.where(i == NPAIR - 1, 1, 0), pl.ds(jnp.minimum(i + 1, NPAIR - 1), 1), :
            ]
            scale = scales(jnp.where(lanes((1, PAIRW)) < HALF, nu, nl))
            lefts.append(left_operand(rot_ref[i] * scale))
        values = [
            product(left, right_ref[i].reshape(2 * PAIRW, SAMP)) for left, i in zip(lefts, index)
        ]
        for i, value in zip(index, values):
            for h, slot in enumerate(next_slots(i)):
                spot = pl.ds(pl.multiple_of((slot % 4) * HALF, HALF), HALF)
                pay_ref[slot // 4, spot, :] = value[h * HALF : (h + 1) * HALF]
        return carry

    lax.fori_loop(0, GROUPS, group, 0)


def step1(norm, operand, rot, parta, partb):
    vmem = pl.BlockSpec(memory_space=pltpu.VMEM)
    return pl.pallas_call(
        step1_kernel,
        in_specs=[vmem, pl.BlockSpec(memory_space=pltpu.HBM), vmem, vmem, vmem],
        out_specs=vmem,
        out_shape=jax.ShapeDtypeStruct((NDEV, PAYROWS, SAMP), F32),
        scratch_shapes=[
            pltpu.VMEM(OPERAND, BF16),
            pltpu.VMEM((2, NPAIR, PAIRW), F32),
            pltpu.SemaphoreType.DMA((GROUPS,)),
        ],
        compiler_params=pltpu.CompilerParams(vmem_limit_bytes=34 * MIB),
        cost_estimate=pl.CostEstimate(flops=3 << 30, bytes_accessed=24 * MIB, transcendentals=0),
        name="step1",
    )(norm, operand, rot, parta, partb)


CHUNK = 4
CHUNKS = NDEV // CHUNK


def parts_kernel(place_ref, y_ref, placed_ref):
    sums = []
    for z_odd in range(2):
        source = [s for s in range(NDEV) if (s // (2 * NX)) % 2 == z_odd]
        sums.append(sum(y_ref[s, 256:PAYROWS, :] for s in source))
    placed_ref[...] = jnp.zeros_like(placed_ref)
    row, core = place_ref[0], place_ref[2]
    spots = [pl.ds(pl.multiple_of(QUARTER * q, QUARTER), QUARTER) for q in (row, core, core + 2)]
    placed_ref[0, spots[0], :] = sums[0][:, :PAIRW] + sums[1][:, :PAIRW]
    placed_ref[1, spots[1], :] = sums[0][:, PAIRW:]
    placed_ref[1, spots[2], :] = sums[1][:, PAIRW:]


def parts(place, y):
    vmem = pl.BlockSpec(memory_space=pltpu.VMEM)
    return pl.pallas_call(
        parts_kernel,
        in_specs=[pl.BlockSpec(memory_space=pltpu.SMEM), vmem],
        out_specs=vmem,
        out_shape=jax.ShapeDtypeStruct((2, 4 * QUARTER, PAIRW), F32),
        compiler_params=pltpu.CompilerParams(vmem_limit_bytes=14 * MIB),
        cost_estimate=pl.CostEstimate(flops=MIB, bytes_accessed=MIB, transcendentals=0),
        name="parts",
    )(place, y)


def gram2_kernel(y_ref, norm_ref, gram_ref):
    totals = [None, None]
    for g in range(CHUNKS):
        source = range(CHUNK * g, CHUNK * (g + 1))
        for j in range(2):
            halves = [split(y_ref[s, j * PAIRW : (j + 1) * PAIRW, :]) for s in source]
            high = jnp.concatenate([h for h, _ in halves], 1)
            low = jnp.concatenate([l for _, l in halves], 1)
            term = outer(high, jnp.concatenate([high, low], 0))
            totals[j] = term if g == 0 else totals[j] + term
    both = []
    for j in range(2):
        mixed = totals[j][:, PAIRW:]
        gram = totals[j][:, :PAIRW] + mixed + mixed.T
        both.append(gram)
        norm_ref[j] = jnp.broadcast_to(diagonal_row(gram), (8, PAIRW))
    gram_ref[...] = jnp.where(upper_or_diagonal(PAIRW), both[0], both[1])


def gram2(y):
    vmem = pl.BlockSpec(memory_space=pltpu.VMEM)
    return pl.pallas_call(
        gram2_kernel,
        in_specs=[vmem],
        out_specs=[vmem, vmem],
        out_shape=[
            jax.ShapeDtypeStruct((2, 8, PAIRW), F32),
            jax.ShapeDtypeStruct((PAIRW, PAIRW), F32),
        ],
        compiler_params=pltpu.CompilerParams(vmem_limit_bytes=14 * MIB),
        cost_estimate=pl.CostEstimate(flops=2 << 30, bytes_accessed=10 * MIB, transcendentals=0),
        name="gram2",
    )(y)


def step2_kernel(norm_ref, rot_ref, y_ref, out_ref, turned_ref, out_sem):
    lefts = [left_operand(rot_ref[j] * scales(norm_ref[j, 0:1])) for j in range(2)]
    for g in range(CHUNKS):
        for j in range(2):
            here = slice(j * PAIRW, (j + 1) * PAIRW)
            for s in range(CHUNK * g, CHUNK * (g + 1)):
                right = jnp.concatenate(split(y_ref[s, here, :]), 0)
                turned_ref[here, s * SAMP : (s + 1) * SAMP] = product(lefts[j], right)
        part = pl.ds(CHUNK * SAMP * g, CHUNK * SAMP)
        pltpu.make_async_copy(turned_ref.at[:, part], out_ref.at[:, part], out_sem).start()
    whole_copy(turned_ref, out_sem).wait()


def step2(norm, rot, y):
    vmem = pl.BlockSpec(memory_space=pltpu.VMEM)
    return pl.pallas_call(
        step2_kernel,
        in_specs=[vmem, vmem, vmem],
        out_specs=pl.BlockSpec(memory_space=pl.ANY),
        out_shape=jax.ShapeDtypeStruct((256, NDEV * SAMP), F32),
        scratch_shapes=[pltpu.VMEM((2 * PAIRW, NDEV * SAMP), F32), pltpu.SemaphoreType.DMA],
        compiler_params=pltpu.CompilerParams(vmem_limit_bytes=24 * MIB),
        cost_estimate=pl.CostEstimate(flops=2 << 30, bytes_accessed=18 * MIB, transcendentals=0),
        name="step2",
    )(norm, rot, y)


def sandwich(mixing_t, gram):
    left = left_operand(mixing_t)
    inner = product(left, jnp.concatenate(split(gram), 0))
    turned = product(left, jnp.concatenate(split(inner.T), 0))
    return turned.T


def grams_kernel(place_ref, norm_ref, norm2_ref, rows_ref, rot1_ref, rot2_ref, out_ref):
    shape = (HALF, PAIRW)
    left = lanes(shape) < HALF
    zero = jnp.zeros(shape, F32)
    keeps = upper_or_diagonal()
    eye = lax.broadcasted_iota(jnp.int32, shape, 0) == lanes(shape)

    def turn(value):
        return pltpu.roll(value, HALF, 1)

    def blocks(both, norm_row):
        other = jnp.concatenate([jnp.where(left, both, zero), zero], 0).T[:HALF]
        lower = jnp.where(keeps, other, both)
        return jnp.where(keeps, both, other), jnp.where(eye, turn(norm_row), lower)

    def symmetric(upper, cross, lower):
        full = jnp.concatenate(
            [jnp.where(left, upper, cross), jnp.where(left, zero, turn(lower))], 0
        )
        low_left = (lanes((PAIRW, PAIRW)) < HALF) & (
            lax.broadcasted_iota(jnp.int32, (PAIRW, PAIRW), 0) >= HALF
        )
        return jnp.where(low_left, full.T, full)

    p = place_ref[5]
    first, last = place_ref[3] == 1, place_ref[4] == 1
    sums = [rows_ref[128:224], rows_ref[224:320]]
    square = rows_ref[:PAIRW]
    above_diagonal = upper_or_diagonal(PAIRW)
    on_diagonal = lax.broadcasted_iota(jnp.int32, square.shape, 0) == lanes(square.shape)
    step2_grams = [
        jnp.where(above_diagonal, square, square.T),
        jnp.where(on_diagonal, norm2_ref[1, 0:1], jnp.where(above_diagonal, square.T, square)),
    ]

    def norm_row(i):
        return norm_ref[pl.ds(i, 1), :]

    own = [blocks(sums[j][:HALF], norm_row(2 * p + j)) for j in range(2)]
    below = blocks(rows_ref[320:384], norm_row(2 * p))[0]
    above = blocks(rows_ref[384:448], norm_row(jnp.minimum(2 * p + 2, NPAIR - 1)))[1]
    uppers = [jnp.where(first, own[0][0], below), jnp.where(first, own[0][1], own[0][0])]
    lowers = [own[1][1], jnp.where(last, own[1][0], above)]
    for j in range(2):
        out_ref[0, j] = symmetric(own[j][0], sums[j][:HALF], own[j][1]) * (1.0 / ROWS)
        packed = sums[j][HALF:]
        gram = symmetric(uppers[j], jnp.concatenate([turn(packed), packed], 0), lowers[j])
        for t, rot, full in (
            (1, rot1_ref[j], gram), (2, rot2_ref[j], step2_grams[j])
        ):
            out_ref[t, j] = sandwich(rot * scales(diagonal_row(full)), full) * (1.0 / ROWS)


def grams(place, norm, norm2, rows, rot1, rot2):
    vmem = pl.BlockSpec(memory_space=pltpu.VMEM)
    return pl.pallas_call(
        grams_kernel,
        in_specs=[pl.BlockSpec(memory_space=pltpu.SMEM)] + [vmem] * 5,
        out_specs=vmem,
        out_shape=jax.ShapeDtypeStruct((3, 2, PAIRW, PAIRW), F32),
        compiler_params=pltpu.CompilerParams(vmem_limit_bytes=16 * MIB),
        cost_estimate=pl.CostEstimate(flops=1 << 20, bytes_accessed=2 * MIB, transcendentals=0),
        name="grams",
    )(place, norm, norm2, rows, rot1, rot2)


def body(samples_slab, block_order, rotations):
    pair, row = lax.axis_index("pair"), lax.axis_index("row")
    core = row % 2
    z_odd = (pair // (NX * 2)) % 2
    place = jnp.stack(
        [row, 2 * z_odd + core, core, pair == 0, pair == NDEV - 1, pair]
    ).astype(jnp.int32)
    even = 2 * jnp.arange(NDEV, dtype=jnp.int32)
    tab = jnp.concatenate([even + core, even + (1 - core)])
    x = samples_slab[0]
    norm0, give, own0, quarter1, turned = norms(x, rotations)
    rot1 = lax.all_gather(quarter1, BOTH, axis=0, tiled=True).reshape(NPAIR, PAIRW, PAIRW)
    copies = spread(own0, norm0, exchange(give, CORE))
    mine = lax.all_to_all(copies, "pair", 0, 0)
    halves = prepare(x)
    mine, halves = together(mine, halves)
    theirs = exchange(mine, CORE)
    norm0 = add_over(collect(mine), YLO)
    operand, given, norm1 = step0(
        tab, block_order, place, norm0, exchange(norm0, CORE), halves, mine, theirs
    )
    kept = given[:2] + exchange(given[2:], CORE)
    norm1 = add_over(norm1, Z1, YLO)
    kept, _ = together(kept, norm1)
    quarters = [kept[0, j] + exchange(kept[1, j], flip) for j, flip in enumerate((YLO, Z1))]
    norm1 = add_over(norm1, CORE, Z3, YBOTH, X1, X3)
    payload = step1(norm1, operand, rot1, *quarters)
    arrived = lax.all_to_all(payload, "pair", 0, 0)
    sums = parts(place, arrived)
    arrived, sums = together(arrived, sums)
    below = lax.ppermute(sums[1, :HALF], "pair", [(k, k + 1) for k in range(NDEV - 1)])
    above = lax.ppermute(sums[0, :HALF], "pair", [(k + 1, k) for k in range(NDEV - 1)])
    norm2, gram = gram2(arrived)
    norm2 = add_over(norm2, CORE)
    rows = [gram, sums.reshape(8 * QUARTER, PAIRW), below, above]
    rows = add_over(jnp.concatenate(rows, 0), CORE)
    norm2 = add_over(norm2, YLO)
    norm2, rows = together(norm2, rows)
    rows = add_over(rows, YLO)
    rotated = step2(norm2, turned[1], arrived)
    return rotated, grams(place, norm1, norm2, rows, turned[0], turned[1])


def solution(mesh):
    in_specs = (P("row", "pair", None), P(), P(None, "pair", None, None))
    out_specs = (P("pair", "row"), P(None, "pair", None, None))
    return jax.shard_map(body, mesh=mesh, in_specs=in_specs, out_specs=out_specs, check_vma=False)
```

```python
import functools
import itertools

import jax
import jax.numpy as jnp
from jax import lax
from jax.experimental import pallas as pl
from jax.experimental.pallas import tpu as pltpu
from jax.sharding import PartitionSpec as P


BOTH = ("pair", "row")
NZ, NX, NY, NC = 4, 4, 2, 2
NPAIR = 64
PAIRW = 128
HALF = 64
SAMP = 256
NDEV = 32
ROWS = 32768
EPS = 1e-06
QUARTER = 24
PAYROWS = 256 + QUARTER
MIB = 1 << 20
F32, BF16 = jnp.float32, jnp.bfloat16


def flat(z, x, yh, yl, c):
    return (((z * NX + x) * 2 + yh) * 2 + yl) * 2 + c


def exchange(value, flip):
    pairs = []
    for here in itertools.product(range(NZ), range(NX), range(2), range(2), range(2)):
        there = tuple(a ^ b for a, b in zip(here, flip))
        pairs.append((flat(*here), flat(*there)))
    return lax.ppermute(value, BOTH, pairs)


X1, X3, Z1, Z3 = (0, 1, 0, 0, 0), (0, 3, 0, 0, 0), (1, 0, 0, 0, 0), (3, 0, 0, 0, 0)
YLO, YBOTH, CORE = (0, 0, 0, 1, 0), (0, 0, 1, 1, 0), (0, 0, 0, 0, 1)


def add_over(value, *flips):
    for flip in flips:
        value = value + exchange(value, flip)
    return value


def together(*values):
    return lax.optimization_barrier(values)


def split(value):
    high = value.astype(BF16)
    return high, (value - high.astype(F32)).astype(BF16)


def left_operand(mixing_t):
    high, low = split(mixing_t)
    return jnp.concatenate(
        [
            jnp.concatenate([high, high], 1),
            jnp.concatenate([low, jnp.zeros_like(low)], 1),
        ],
        0,
    )


def product(left, right):
    wide = jnp.dot(left, right, preferred_element_type=F32)
    return wide[:PAIRW] + wide[PAIRW:]


def outer(a, b):
    return lax.dot_general(a, b, (((1,), (1,)), ((), ())), preferred_element_type=F32)


def self_gram(stacked):
    wide = outer(stacked, stacked)
    return wide[:PAIRW, :PAIRW] + wide[PAIRW:, :PAIRW] + wide[:PAIRW, PAIRW:]


def diagonal_row(gram):
    size = gram.shape[0]
    eye = lax.broadcasted_iota(jnp.int32, (size, size), 0) == lax.broadcasted_iota(
        jnp.int32, (size, size), 1
    )
    return jnp.sum(jnp.where(eye, gram, 0.0), axis=0, keepdims=True)


def scales(norm_row):
    return lax.rsqrt(norm_row / ROWS + EPS)


def lanes(shape):
    return lax.broadcasted_iota(jnp.int32, shape, 1)


def upper_or_diagonal(rows=HALF):
    shape = (rows, PAIRW)
    return lax.broadcasted_iota(jnp.int32, shape, 0) <= lanes(shape)


def next_slots(i):
    upper = jnp.where(i == 0, 0, jnp.where(i == NPAIR - 1, 2 * NPAIR - 1, 2 * i + 2))
    lower = jnp.where(i == 0, 2, 2 * i - 1)
    return upper, lower


TILES = NPAIR // 2


def norms_kernel(
    x_ref, rotations_ref, keep_ref, give_ref, own_ref, quarter_ref, turned_ref,
    held_ref, rot_ref, rows_ref, sems, rot_sem
):
    count = sems.shape[0]
    width = NPAIR // count

    def copy(g):
        part = pl.ds(g * width * PAIRW, width * PAIRW)
        return pltpu.make_async_copy(x_ref.at[:, part], held_ref.at[:, part], sems.at[g])

    rot_copy = pltpu.make_async_copy(rotations_ref, rot_ref, rot_sem)
    rot_copy.start()
    for g in range(count):
        copy(g).start()
    row = lax.axis_index("row")
    core = lax.rem(row, 2)
    rot_copy.wait()
    own_ref[...] = rot_ref[0, core].T
    for t in range(1, 3):
        for j in range(2):
            turned_ref[t - 1, j] = rot_ref[t, j].T
    half = pl.ds(pl.multiple_of(core * HALF, HALF), HALF)
    quarter_ref[...] = turned_ref[0, lax.div(row, 2), half, :]
    for g in range(count):
        copy(g).wait()
        for t in range(width * g, width * (g + 1)):
            tile = held_ref[:, t * PAIRW : (t + 1) * PAIRW]
            rows_ref[t // TILES, t % TILES : t % TILES + 1, :] = jnp.sum(
                tile * tile, axis=0, keepdims=True
            )
    keep_ref[...] = rows_ref[core]
    give_ref[...] = rows_ref[1 - core]


def norms(x, rotations):
    vmem = pl.BlockSpec(memory_space=pltpu.VMEM)
    hbm = pl.BlockSpec(memory_space=pltpu.HBM)
    return pl.pallas_call(
        norms_kernel,
        in_specs=[hbm, hbm],
        out_specs=[vmem] * 5,
        out_shape=[
            jax.ShapeDtypeStruct((TILES, PAIRW), F32),
            jax.ShapeDtypeStruct((TILES, PAIRW), F32),
            jax.ShapeDtypeStruct((PAIRW, PAIRW), F32),
            jax.ShapeDtypeStruct((HALF, PAIRW), F32),
            jax.ShapeDtypeStruct((2, 2, PAIRW, PAIRW), F32),
        ],
        scratch_shapes=[
            pltpu.VMEM((SAMP, NPAIR * PAIRW), F32),
            pltpu.VMEM((3, 2, PAIRW, PAIRW), F32),
            pltpu.VMEM((2, TILES, PAIRW), F32),
            pltpu.SemaphoreType.DMA((16,)),
            pltpu.SemaphoreType.DMA,
        ],
        compiler_params=pltpu.CompilerParams(vmem_limit_bytes=58 * MIB),
        cost_estimate=pl.CostEstimate(flops=8 * MIB, bytes_accessed=8 * MIB, transcendentals=0),
        name="norms",
    )(x, rotations)


def prepare_kernel(x_ref, halves_ref):
    tiles = x_ref.shape[1] // PAIRW
    for t in range(tiles):
        tile = x_ref[:, t * PAIRW : (t + 1) * PAIRW]
        high, low = split(tile.T)
        for h in range(2):
            halves_ref[2 * t + h, 0] = high[h * HALF : (h + 1) * HALF]
            halves_ref[2 * t + h, 1] = low[h * HALF : (h + 1) * HALF]


def prepare(x):
    width = 1024
    blocks = width // HALF
    return pl.pallas_call(
        prepare_kernel,
        grid=(x.shape[1] // width,),
        in_specs=[pl.BlockSpec((SAMP, width), lambda g: (0, g))],
        out_specs=pl.BlockSpec((blocks, 2, HALF, SAMP), lambda g: (g, 0, 0, 0)),
        out_shape=jax.ShapeDtypeStruct((2 * NPAIR, 2, HALF, SAMP), BF16),
        compiler_params=pltpu.CompilerParams(vmem_limit_bytes=58 * MIB),
        cost_estimate=pl.CostEstimate(flops=MIB, bytes_accessed=MIB // 8, transcendentals=0),
        name="prepare",
    )(x)


SENT = PAIRW + TILES


def spread_kernel(own_ref, norm_ref, given_ref, copies_ref):
    own = own_ref[...]
    norm = norm_ref[...] + given_ref[...]

    def copy(k, carry):
        copies_ref[k, :PAIRW] = own
        copies_ref[k, PAIRW:] = norm
        return carry

    lax.fori_loop(0, NDEV, copy, 0, unroll=4)


def spread(own, norm, given):
    vmem = pl.BlockSpec(memory_space=pltpu.VMEM)
    return pl.pallas_call(
        spread_kernel,
        in_specs=[vmem] * 3,
        out_specs=vmem,
        out_shape=jax.ShapeDtypeStruct((NDEV, SENT, PAIRW), F32),
        compiler_params=pltpu.CompilerParams(vmem_limit_bytes=58 * MIB),
        cost_estimate=pl.CostEstimate(flops=MIB, bytes_accessed=MIB // 8, transcendentals=0),
        name="spread",
    )(own, norm, given)


def collect_kernel(arrived_ref, norm_ref):
    norm_ref[...] = sum(arrived_ref[s, PAIRW:] for s in range(NDEV))


def collect(arrived):
    vmem = pl.BlockSpec(memory_space=pltpu.VMEM)
    return pl.pallas_call(
        collect_kernel,
        in_specs=[vmem],
        out_specs=vmem,
        out_shape=jax.ShapeDtypeStruct((TILES, PAIRW), F32),
        compiler_params=pltpu.CompilerParams(vmem_limit_bytes=8 * MIB),
        cost_estimate=pl.CostEstimate(flops=MIB, bytes_accessed=MIB // 8, transcendentals=0),
        name="collect",
    )(arrived)


GROUP = 16
GROUPS = NPAIR // GROUP
OPERAND = (NPAIR, 2, 2, HALF, SAMP)
ROOM = 4


def whole_copy(ref, sem):
    return pltpu.make_async_copy(ref, ref, sem)


def step0_kernel(
    tab_ref, order_ref, place_ref, normc_ref, normo_ref, halves_ref, mine_ref, given_ref,
    next_ref, parts_ref, onorm_ref, right_ref, rot_ref, moved_ref, norms_ref, sems, out_sem
):

    def fetch(q, carry):
        i = tab_ref[q]
        for h in range(2):
            pltpu.make_async_copy(
                halves_ref.at[order_ref[2 * i + h]], right_ref.at[q, :, h], sems.at[0, q // GROUP]
            ).start()
        return carry

    lax.fori_loop(0, NPAIR, fetch, 0)
    for k in range(GROUPS):
        source, first = divmod(GROUP * k, NDEV)
        piece = (mine_ref, given_ref)[source].at[pl.ds(first, GROUP), pl.ds(0, PAIRW)]
        pltpu.make_async_copy(piece, rot_ref.at[pl.ds(GROUP * k, GROUP)], sems.at[1, k]).start()

    core = place_ref[2]
    for half, norm_ref in ((core, normc_ref), (1 - core, normo_ref)):
        rows = pl.ds(pl.multiple_of(half * TILES, TILES), TILES)
        norms_ref[0, rows, :] = norm_ref[...]
        norms_ref[1, rows, :] = pltpu.roll(norm_ref[...], HALF, 1)

    def spot(quarter, j):
        mine = quarter ^ place_ref[j]
        return (mine & 1) * 2 + (mine >> 1)

    def group(g, carry):
        part = pl.ds(GROUP * g, GROUP)
        whole_copy(right_ref.at[part], sems.at[0, g]).wait()
        whole_copy(rot_ref.at[part], sems.at[1, g]).wait()
        todo = [GROUP * g + k for k in range(GROUP)]
        index = [tab_ref[q] for q in todo]
        lefts = []
        for q, i in zip(todo, index):
            bu, bl = order_ref[2 * i], order_ref[2 * i + 1]
            nu = norms_ref[bu % 2, pl.ds(bu // 2, 1), :]
            nl = norms_ref[1 - bl % 2, pl.ds(bl // 2, 1), :]
            scale = scales(jnp.where(lanes((1, PAIRW)) < HALF, nu, nl))
            lefts.append(left_operand(rot_ref[q] * scale))
        values = [
            split(product(left, right_ref[q].reshape(2 * PAIRW, SAMP)))
            for left, q in zip(lefts, todo)
        ]
        for i, pieces_of in zip(index, values):
            slots = next_slots(i)
            for part_of, value in enumerate(pieces_of):
                for h, slot in enumerate(slots):
                    moved_ref[slot // 2, part_of, slot % 2] = value[h * HALF : (h + 1) * HALF]
        for i, (high, low) in zip(index, values):
            gram = self_gram(jnp.concatenate([high, low], 0))
            onorm_ref[pl.ds(i, 1), :] = diagonal_row(gram)
            both = jnp.where(upper_or_diagonal(), gram[:HALF], pltpu.roll(gram[HALF:], HALF, 1))
            both = jnp.where(lanes((HALF, PAIRW)) < HALF, both, gram[:HALF])
            p, j = i // 2, i % 2
            parts_ref[spot(0, j), j, p] = both[0:24]
            parts_ref[spot(1, j), j, p] = both[24:48]
            parts_ref[spot(2, j), j, p, 0:16] = both[48:64]
        return carry

    lax.fori_loop(0, GROUPS, group, 0)

    copy = pltpu.make_async_copy(moved_ref, next_ref.at[pl.ds(0, NPAIR)], out_sem)
    copy.start()

    def cross(g, carry):
        wides = []
        for k in range(GROUP):
            upper = moved_ref[GROUP * g + k, :, 0].reshape(PAIRW, SAMP)
            lower = moved_ref[GROUP * g + k, :, 1].reshape(PAIRW, SAMP)
            wides.append(outer(upper, lower))
        for k, wide in enumerate(wides):
            folded = wide[:HALF] + wide[HALF:]
            folded = folded + pltpu.roll(folded, HALF, 1)
            packed = jnp.where(lanes((32, PAIRW)) < HALF, folded[:32], folded[32:])
            p, j = GROUP // 2 * g + k // 2, k % 2
            parts_ref[spot(2, j), j, p, 16:24] = packed[:8]
            parts_ref[spot(3, j), j, p] = packed[8:]
        return carry

    lax.fori_loop(0, GROUPS, cross, 0)
    copy.wait()


def step0(tab, order, place, normc, normo, halves, mine, given):
    smem = pl.BlockSpec(memory_space=pltpu.SMEM)
    vmem = pl.BlockSpec(memory_space=pltpu.VMEM)
    hbm = pl.BlockSpec(memory_space=pltpu.HBM)
    return pl.pallas_call(
        step0_kernel,
        in_specs=[smem] * 3 + [vmem] * 2 + [hbm] * 3,
        out_specs=[hbm, vmem, vmem],
        out_shape=[
            jax.ShapeDtypeStruct((ROOM * NPAIR,) + OPERAND[1:], BF16),
            jax.ShapeDtypeStruct((4, 2, NDEV, QUARTER, PAIRW), F32),
            jax.ShapeDtypeStruct((NPAIR, PAIRW), F32),
        ],
        scratch_shapes=[
            pltpu.VMEM(OPERAND, BF16),
            pltpu.VMEM((NPAIR, PAIRW, PAIRW), F32),
            pltpu.VMEM(OPERAND, BF16),
            pltpu.VMEM((2, NPAIR, PAIRW), F32),
            pltpu.SemaphoreType.DMA((2, GROUPS)),
            pltpu.SemaphoreType.DMA,
        ],
        compiler_params=pltpu.CompilerParams(vmem_limit_bytes=44 * MIB),
        cost_estimate=pl.CostEstimate(flops=MIB, bytes_accessed=MIB // 8, transcendentals=0),
        name="step0",
    )(tab, order, place, normc, normo, halves, mine, given)


def step1_kernel(
    norm_ref, operand_ref, rot_ref, parta_ref, partb_ref, pay_ref, right_ref, norms_ref, sems
):
    for g in range(GROUPS):
        part = pl.ds(GROUP * g, GROUP)
        pltpu.make_async_copy(operand_ref.at[part], right_ref.at[part], sems.at[g]).start()
    norms_ref[0] = norm_ref[...]
    norms_ref[1] = pltpu.roll(norm_ref[...], HALF, 1)
    pay_ref[:, 256:PAYROWS, :PAIRW] = parta_ref[...]
    pay_ref[:, 256:PAYROWS, PAIRW:] = partb_ref[...]

    def group(g, carry):
        whole_copy(right_ref.at[pl.ds(GROUP * g, GROUP)], sems.at[g]).wait()
        index = [GROUP * g + k for k in range(GROUP)]
        lefts = []
        for i in index:
            nu = norms_ref[jnp.where(i == 1, 1, 0), pl.ds(jnp.maximum(i - 1, 0), 1), :]
            nl = norms_ref[
                jnp.where(i == NPAIR - 1, 1, 0), pl.ds(jnp.minimum(i + 1, NPAIR - 1), 1), :
            ]
            scale = scales(jnp.where(lanes((1, PAIRW)) < HALF, nu, nl))
            lefts.append(left_operand(rot_ref[i] * scale))
        values = [
            product(left, right_ref[i].reshape(2 * PAIRW, SAMP)) for left, i in zip(lefts, index)
        ]
        for i, value in zip(index, values):
            for h, slot in enumerate(next_slots(i)):
                spot = pl.ds(pl.multiple_of((slot % 4) * HALF, HALF), HALF)
                pay_ref[slot // 4, spot, :] = value[h * HALF : (h + 1) * HALF]
        return carry

    lax.fori_loop(0, GROUPS, group, 0)


def step1(norm, operand, rot, parta, partb):
    vmem = pl.BlockSpec(memory_space=pltpu.VMEM)
    return pl.pallas_call(
        step1_kernel,
        in_specs=[vmem, pl.BlockSpec(memory_space=pltpu.HBM), vmem, vmem, vmem],
        out_specs=vmem,
        out_shape=jax.ShapeDtypeStruct((NDEV, PAYROWS, SAMP), F32),
        scratch_shapes=[
            pltpu.VMEM(OPERAND, BF16),
            pltpu.VMEM((2, NPAIR, PAIRW), F32),
            pltpu.SemaphoreType.DMA((GROUPS,)),
        ],
        compiler_params=pltpu.CompilerParams(vmem_limit_bytes=34 * MIB),
        cost_estimate=pl.CostEstimate(flops=3 << 30, bytes_accessed=24 * MIB, transcendentals=0),
        name="step1",
    )(norm, operand, rot, parta, partb)


CHUNK = 4
CHUNKS = NDEV // CHUNK


def parts_kernel(place_ref, y_ref, placed_ref):
    sums = []
    for z_odd in range(2):
        source = [s for s in range(NDEV) if (s // (2 * NX)) % 2 == z_odd]
        sums.append(sum(y_ref[s, 256:PAYROWS, :] for s in source))
    placed_ref[...] = jnp.zeros_like(placed_ref)
    row, core = place_ref[0], place_ref[2]
    spots = [pl.ds(pl.multiple_of(QUARTER * q, QUARTER), QUARTER) for q in (row, core, core + 2)]
    placed_ref[0, spots[0], :] = sums[0][:, :PAIRW] + sums[1][:, :PAIRW]
    placed_ref[1, spots[1], :] = sums[0][:, PAIRW:]
    placed_ref[1, spots[2], :] = sums[1][:, PAIRW:]


def parts(place, y):
    vmem = pl.BlockSpec(memory_space=pltpu.VMEM)
    return pl.pallas_call(
        parts_kernel,
        in_specs=[pl.BlockSpec(memory_space=pltpu.SMEM), vmem],
        out_specs=vmem,
        out_shape=jax.ShapeDtypeStruct((2, 4 * QUARTER, PAIRW), F32),
        compiler_params=pltpu.CompilerParams(vmem_limit_bytes=14 * MIB),
        cost_estimate=pl.CostEstimate(flops=MIB, bytes_accessed=MIB, transcendentals=0),
        name="parts",
    )(place, y)


def gram2_kernel(y_ref, norm_ref, gram_ref):
    totals = [None, None]
    for g in range(CHUNKS):
        source = range(CHUNK * g, CHUNK * (g + 1))
        for j in range(2):
            halves = [split(y_ref[s, j * PAIRW : (j + 1) * PAIRW, :]) for s in source]
            high = jnp.concatenate([h for h, _ in halves], 1)
            low = jnp.concatenate([l for _, l in halves], 1)
            term = outer(high, jnp.concatenate([high, low], 0))
            totals[j] = term if g == 0 else totals[j] + term
    both = []
    for j in range(2):
        mixed = totals[j][:, PAIRW:]
        gram = totals[j][:, :PAIRW] + mixed + mixed.T
        both.append(gram)
        norm_ref[j] = jnp.broadcast_to(diagonal_row(gram), (8, PAIRW))
    gram_ref[...] = jnp.where(upper_or_diagonal(PAIRW), both[0], both[1])


def gram2(y):
    vmem = pl.BlockSpec(memory_space=pltpu.VMEM)
    return pl.pallas_call(
        gram2_kernel,
        in_specs=[vmem],
        out_specs=[vmem, vmem],
        out_shape=[
            jax.ShapeDtypeStruct((2, 8, PAIRW), F32),
            jax.ShapeDtypeStruct((PAIRW, PAIRW), F32),
        ],
        compiler_params=pltpu.CompilerParams(vmem_limit_bytes=14 * MIB),
        cost_estimate=pl.CostEstimate(flops=2 << 30, bytes_accessed=10 * MIB, transcendentals=0),
        name="gram2",
    )(y)


def step2_kernel(norm_ref, rot_ref, y_ref, out_ref, turned_ref, out_sem):
    lefts = [left_operand(rot_ref[j] * scales(norm_ref[j, 0:1])) for j in range(2)]
    for g in range(CHUNKS):
        for j in range(2):
            here = slice(j * PAIRW, (j + 1) * PAIRW)
            for s in range(CHUNK * g, CHUNK * (g + 1)):
                right = jnp.concatenate(split(y_ref[s, here, :]), 0)
                turned_ref[here, s * SAMP : (s + 1) * SAMP] = product(lefts[j], right)
        part = pl.ds(CHUNK * SAMP * g, CHUNK * SAMP)
        pltpu.make_async_copy(turned_ref.at[:, part], out_ref.at[:, part], out_sem).start()
    whole_copy(turned_ref, out_sem).wait()


def step2(norm, rot, y):
    vmem = pl.BlockSpec(memory_space=pltpu.VMEM)
    return pl.pallas_call(
        step2_kernel,
        in_specs=[vmem, vmem, vmem],
        out_specs=pl.BlockSpec(memory_space=pl.ANY),
        out_shape=jax.ShapeDtypeStruct((256, NDEV * SAMP), F32),
        scratch_shapes=[pltpu.VMEM((2 * PAIRW, NDEV * SAMP), F32), pltpu.SemaphoreType.DMA],
        compiler_params=pltpu.CompilerParams(vmem_limit_bytes=24 * MIB),
        cost_estimate=pl.CostEstimate(flops=2 << 30, bytes_accessed=18 * MIB, transcendentals=0),
        name="step2",
    )(norm, rot, y)


def sandwich(mixing_t, gram):
    left = left_operand(mixing_t)
    inner = product(left, jnp.concatenate(split(gram), 0))
    turned = product(left, jnp.concatenate(split(inner.T), 0))
    return turned.T


def grams_kernel(place_ref, norm_ref, norm2_ref, rows_ref, rot1_ref, rot2_ref, out_ref):
    shape = (HALF, PAIRW)
    left = lanes(shape) < HALF
    zero = jnp.zeros(shape, F32)
    keeps = upper_or_diagonal()
    eye = lax.broadcasted_iota(jnp.int32, shape, 0) == lanes(shape)

    def turn(value):
        return pltpu.roll(value, HALF, 1)

    def blocks(both, norm_row):
        other = jnp.concatenate([jnp.where(left, both, zero), zero], 0).T[:HALF]
        lower = jnp.where(keeps, other, both)
        return jnp.where(keeps, both, other), jnp.where(eye, turn(norm_row), lower)

    def symmetric(upper, cross, lower):
        full = jnp.concatenate(
            [jnp.where(left, upper, cross), jnp.where(left, zero, turn(lower))], 0
        )
        low_left = (lanes((PAIRW, PAIRW)) < HALF) & (
            lax.broadcasted_iota(jnp.int32, (PAIRW, PAIRW), 0) >= HALF
        )
        return jnp.where(low_left, full.T, full)

    p = place_ref[5]
    first, last = place_ref[3] == 1, place_ref[4] == 1
    sums = [rows_ref[128:224], rows_ref[224:320]]
    square = rows_ref[:PAIRW]
    above_diagonal = upper_or_diagonal(PAIRW)
    on_diagonal = lax.broadcasted_iota(jnp.int32, square.shape, 0) == lanes(square.shape)
    step2_grams = [
        jnp.where(above_diagonal, square, square.T),
        jnp.where(on_diagonal, norm2_ref[1, 0:1], jnp.where(above_diagonal, square.T, square)),
    ]

    def norm_row(i):
        return norm_ref[pl.ds(i, 1), :]

    own = [blocks(sums[j][:HALF], norm_row(2 * p + j)) for j in range(2)]
    below = blocks(rows_ref[320:384], norm_row(2 * p))[0]
    above = blocks(rows_ref[384:448], norm_row(jnp.minimum(2 * p + 2, NPAIR - 1)))[1]
    uppers = [jnp.where(first, own[0][0], below), jnp.where(first, own[0][1], own[0][0])]
    lowers = [own[1][1], jnp.where(last, own[1][0], above)]
    for j in range(2):
        out_ref[0, j] = symmetric(own[j][0], sums[j][:HALF], own[j][1]) * (1.0 / ROWS)
        packed = sums[j][HALF:]
        gram = symmetric(uppers[j], jnp.concatenate([turn(packed), packed], 0), lowers[j])
        for t, rot, full in (
            (1, rot1_ref[j], gram), (2, rot2_ref[j], step2_grams[j])
        ):
            out_ref[t, j] = sandwich(rot * scales(diagonal_row(full)), full) * (1.0 / ROWS)


def grams(place, norm, norm2, rows, rot1, rot2):
    vmem = pl.BlockSpec(memory_space=pltpu.VMEM)
    return pl.pallas_call(
        grams_kernel,
        in_specs=[pl.BlockSpec(memory_space=pltpu.SMEM)] + [vmem] * 5,
        out_specs=vmem,
        out_shape=jax.ShapeDtypeStruct((3, 2, PAIRW, PAIRW), F32),
        compiler_params=pltpu.CompilerParams(vmem_limit_bytes=16 * MIB),
        cost_estimate=pl.CostEstimate(flops=1 << 20, bytes_accessed=2 * MIB, transcendentals=0),
        name="grams",
    )(place, norm, norm2, rows, rot1, rot2)


def body(samples_slab, block_order, rotations):
    pair, row = lax.axis_index("pair"), lax.axis_index("row")
    core = row % 2
    z_odd = (pair // (NX * 2)) % 2
    place = jnp.stack(
        [row, 2 * z_odd + core, core, pair == 0, pair == NDEV - 1, pair]
    ).astype(jnp.int32)
    even = 2 * jnp.arange(NDEV, dtype=jnp.int32)
    tab = jnp.concatenate([even + core, even + (1 - core)])
    x = samples_slab[0]
    norm0, give, own0, quarter1, turned = norms(x, rotations)
    rot1 = lax.all_gather(quarter1, BOTH, axis=0, tiled=True).reshape(NPAIR, PAIRW, PAIRW)
    copies = spread(own0, norm0, exchange(give, CORE))
    mine = lax.all_to_all(copies, "pair", 0, 0)
    halves = prepare(x)
    mine, halves = together(mine, halves)
    theirs = exchange(mine, CORE)
    norm0 = add_over(collect(mine), YLO)
    operand, given, norm1 = step0(
        tab, block_order, place, norm0, exchange(norm0, CORE), halves, mine, theirs
    )
    kept = given[:2] + exchange(given[2:], CORE)
    norm1 = add_over(norm1, Z1, YLO)
    kept, _ = together(kept, norm1)
    quarters = [kept[0, j] + exchange(kept[1, j], flip) for j, flip in enumerate((YLO, Z1))]
    norm1 = add_over(norm1, CORE, Z3, YBOTH, X1, X3)
    payload = step1(norm1, operand, rot1, *quarters)
    arrived = lax.all_to_all(payload, "pair", 0, 0)
    sums = parts(place, arrived)
    arrived, sums = together(arrived, sums)
    below = lax.ppermute(sums[1, :HALF], "pair", [(k, k + 1) for k in range(NDEV - 1)])
    above = lax.ppermute(sums[0, :HALF], "pair", [(k + 1, k) for k in range(NDEV - 1)])
    norm2, gram = gram2(arrived)
    norm2 = add_over(norm2, CORE)
    rows = [gram, sums.reshape(8 * QUARTER, PAIRW), below, above]
    rows = add_over(jnp.concatenate(rows, 0), CORE)
    norm2 = add_over(norm2, YLO)
    norm2, rows = together(norm2, rows)
    rows = add_over(rows, YLO)
    rotated = step2(norm2, turned[1], arrived)
    return rotated, grams(place, norm1, norm2, rows, turned[0], turned[1])


def solution(mesh):
    in_specs = (P("row", "pair", None), P(), P(None, "pair", None, None))
    out_specs = (P("pair", "row"), P(None, "pair", None, None))
    return jax.shard_map(body, mesh=mesh, in_specs=in_specs, out_specs=out_specs, check_vma=False)
```
